512 devices in a mesh: rep: 16 (over z_lo, x), row: 32 (over z_hi, y, core).
Axes of the slice: x: 4, y: 4, z: 16 (z_hi: 4, z_lo: 4; z = z_hi * 4 + z_lo), core: 2. Of those that a mesh axis runs over, the one named last changes fastest.
Arguments:
- features: bfloat16 [32768, 128], P('row'), may hold values from -6 to 6
- tile_values: bfloat16 [16, 32, 96, 128, 128], P('rep', 'row'), may hold values from 0 to 0.079589844
- tile_counts: int32 [16, 32, 8], P('rep', 'row'), may hold values from 1 to 12, as said below
- tile_columns: int32 [16, 32, 96], P('rep', 'row'), may hold values from 0 to 15, as said below
- weight: bfloat16 [128, 256], replicated, may hold values from -0.5 to 0.5
- node_grad: bfloat16 [32768, 256], P('row'), may hold values from -6 to 6
Outputs:
- output: bfloat16 [32768, 256], P('row')
- weight_grad: float32 [128, 256], replicated
- feature_grad: bfloat16 [32768, 128], P('row')
The draws below stay inside these ranges and needn't reach their ends.
Inputs may be any that keep to these rules, and one draw needn't show every extreme that they name: `tile_counts`: each entry counts the live tiles of one row block among the 16 column blocks of its replica group; in every draw some node shard of some replica group has 12 in all its 8 row blocks. `tile_columns`: within the live slots of one row block the columns are distinct; slots past a device's total count are not live and hold any column.
All inputs are finite; a program needn't handle non-finite values.
Results may differ from the reference program's by a relative error of at most 0.005.
Values may be sent and summed in bfloat16 or wider, within the bound.
No kernel may reach another device: no remote copies, remote signals or barrier semaphores. Data moves between devices by JAX's collectives and lax.ppermute only.
A program may use at most 64 MiB of HBM per device.

```python
import math
import jax
import jax.numpy as jnp
from jax import lax

TILE = 128
F_IN = 128
F_OUT = 256
BLK_DEV = 8
COLS = 16
TILES_BLK = 12
MAXT = 96
NODES = 32768
N_REP = 16
N_ROW = 32


def make_counts(key):
    base = jax.random.fold_in(key, 11)
    key_level, key_raw, key_full = jax.random.split(base, 3)
    levels = jax.random.randint(key_level, (N_REP, N_ROW, 1), 1, TILES_BLK + 1)
    raw_draw = jax.random.randint(key_raw, (N_REP, N_ROW, BLK_DEV), 0, 1 << 20)
    counts = 1 + raw_draw % levels
    full_device = jax.random.randint(key_full, (), 0, N_REP * N_ROW)
    device_ids = jnp.arange(N_REP * N_ROW, dtype=jnp.int32).reshape(N_REP, N_ROW, 1)
    counts = jnp.where(device_ids == full_device, TILES_BLK, counts)
    return counts.astype(jnp.int32)


def draw_tile_counts(key, part):
    return make_counts(key)


def draw_tile_columns(key, part):
    counts = make_counts(key)
    key = jax.random.fold_in(key, 5)
    scores = jax.random.randint(key, (N_REP, N_ROW, BLK_DEV, COLS), 0, 1 << 20)
    scores = scores * COLS + jnp.arange(COLS, dtype=jnp.int32)
    orders = jnp.argsort(scores, axis=-1, stable=True).astype(jnp.int32)
    block_ends = jnp.cumsum(counts, axis=-1)
    block_starts = block_ends - counts
    slot_ids = jnp.arange(MAXT, dtype=jnp.int32)
    local_block = jnp.sum((slot_ids[None, None, :, None] >= block_ends[:, :, None, :]).astype(jnp.int32), axis=-1)
    local_block = jnp.minimum(local_block, BLK_DEV - 1)
    slot_start = jnp.take_along_axis(block_starts, local_block, axis=-1)
    offsets = (slot_ids[None, None, :] - slot_start) % COLS
    flat_orders = orders.reshape(N_REP, N_ROW, BLK_DEV * COLS)
    columns = jnp.take_along_axis(flat_orders, local_block * COLS + offsets, axis=-1)
    return columns.astype(jnp.int32)


def block_scale(key, shape, cuts, smallest, top_value):
    level, own = 1.0, jax.random.fold_in(key, 6)
    for position, blocks in cuts:
        steps = jnp.exp(jax.random.uniform(jax.random.fold_in(own, position), (blocks,), jnp.float32, smallest / len(cuts), top_value / len(cuts)))
        level = level * jnp.repeat(steps, shape[position] // blocks).reshape([-1 if axis == position else 1 for axis in range(len(shape))])
    return level


def normal_values(stream_key, shape, width, bound, cuts=(), held_as=jnp.bfloat16):
    factor_of = block_scale(stream_key, shape, cuts, -0.22, 0.18) if cuts else 1.0
    result = jax.random.normal(stream_key, shape, jnp.float32) * width * factor_of
    return jnp.minimum(jnp.maximum(result, -bound), bound).astype(held_as)


def setup_inputs(seed: int = 0) -> dict:
    key_of = jax.random.split(jax.random.key(seed), 7)
    return {
        "features": normal_values(key_of[0], (NODES, F_IN), 1.0, 6.0, ((0, 32),)),
        "tile_values": jnp.clip(0.079589844 * jax.random.uniform(key_of[1], (N_REP, N_ROW, MAXT, TILE, TILE), jnp.float32) ** block_scale(key_of[1], (N_REP, N_ROW, MAXT, TILE, TILE), ((0, 16), (1, 32)), -0.2, 0.2), 0.0, 0.079589844).astype(jnp.bfloat16),
        "tile_counts": draw_tile_counts(jax.random.fold_in(key_of[6], 71), 0),
        "tile_columns": draw_tile_columns(jax.random.fold_in(key_of[6], 71), 0),
        "weight": normal_values(key_of[4], (F_IN, F_OUT), F_IN ** -0.5, 0.5),
        "node_grad": normal_values(key_of[5], (NODES, F_OUT), 1.0, 6.0, ((0, 32),)),
    }


def reference(features, tile_values, tile_counts, tile_columns, weight, node_grad):
    device_total = N_REP * N_ROW
    tile_vals = tile_values.reshape(device_total, MAXT, TILE, TILE)
    count_rows = tile_counts.reshape(device_total, BLK_DEV)
    col_rows = tile_columns.reshape(device_total, MAXT)
    device_ids = jnp.arange(device_total, dtype=jnp.int32)
    slot_ids = jnp.arange(MAXT, dtype=jnp.int32)
    blocks = jnp.arange(BLK_DEV, dtype=jnp.int32)
    feat_blocks = features.reshape(N_ROW * BLK_DEV, TILE, F_IN)

    def layout(count_row, col_row, device):
        block_ends = jnp.cumsum(count_row)
        local_block = lax.optimization_barrier(jnp.sum((slot_ids[:, None] >= block_ends[None, :]).astype(jnp.int32), axis=1))
        local_block = jnp.minimum(local_block, BLK_DEV - 1).astype(jnp.int32)
        live_mask = (slot_ids < block_ends[BLK_DEV - 1]).astype(jnp.float32)
        rep_index = device // N_ROW
        row_index = device % N_ROW
        owner_row = col_row // BLK_DEV * N_REP + rep_index
        global_col = (owner_row * BLK_DEV + col_row % BLK_DEV).astype(jnp.int32)
        global_row = (row_index * BLK_DEV + local_block).astype(jnp.int32)
        return (local_block, global_row, global_col, live_mask)

    def forward_one(record):
        tile_block, count_row, col_row, device = record
        local_block, global_row, global_col, live_mask = layout(count_row, col_row, device)
        picked = feat_blocks[global_col].astype(jnp.float32)
        products = jnp.einsum('tij,tjf->tif', tile_block.astype(jnp.float32), picked)
        products = products * live_mask[:, None, None]
        onehot = (local_block[None, :] == blocks[:, None]).astype(jnp.float32)
        return jnp.einsum('bt,tif->bif', onehot, products, precision=lax.Precision.HIGHEST)
    partials = lax.map(forward_one, (tile_vals, count_rows, col_rows, device_ids))
    aggregate = lax.optimization_barrier(jnp.sum(partials.reshape(N_REP, NODES, F_IN), axis=0)).astype(jnp.bfloat16)
    output = jnp.dot(aggregate, weight, preferred_element_type=jnp.float32).astype(jnp.bfloat16)
    weight_grad = jnp.dot(aggregate.T, node_grad, preferred_element_type=jnp.float32) / math.sqrt(NODES)
    grad_rows = jnp.dot(node_grad, weight.T, preferred_element_type=jnp.float32).astype(jnp.bfloat16)
    grad_blocks = grad_rows.reshape(N_ROW * BLK_DEV, TILE, F_IN)

    def backward_one(accumulated, record):
        tile_block, count_row, col_row, device = record
        local_block, global_row, global_col, live_mask = layout(count_row, col_row, device)
        picked = grad_blocks[global_row].astype(jnp.float32)
        backward = jnp.einsum('tji,tjf->tif', tile_block.astype(jnp.float32), picked)
        backward = backward * live_mask[:, None, None]
        return (accumulated.at[global_col].add(backward), None)
    start_value = jnp.zeros((N_ROW * BLK_DEV, TILE, F_IN), jnp.float32)
    accumulated, unused = lax.scan(backward_one, start_value, (tile_vals, count_rows, col_rows, device_ids))
    feature_grad = accumulated.reshape(NODES, F_IN).astype(jnp.bfloat16)
    return (output, weight_grad, feature_grad)
```

```python
import math

import jax
import jax.numpy as jnp
from jax import lax
from jax.experimental import pallas as pl
from jax.experimental.pallas import tpu as pltpu
from jax.sharding import Mesh
from jax.sharding import PartitionSpec as P

REP = ("zl", "x")
ROW = ("zh", "y", "c")
YC = ("y", "c")
F32 = jnp.float32
BF16 = jnp.bfloat16
VMEM = pl.BlockSpec(memory_space=pltpu.VMEM)
SMEM = pl.BlockSpec(memory_space=pltpu.SMEM)
PARAMS = pltpu.CompilerParams(vmem_limit_bytes=40 * 1024 * 1024)

PAIRS = [
    ((zh * 4 + k % 4) * 32 + q + 16 * (k // 4), q * 32 + zh * 8 + k)
    for q in range(16)
    for zh in range(4)
    for k in range(8)
]


def split_high_low(value):
    high = value.astype(BF16)
    return high, (value - high.astype(F32)).astype(BF16)


def backward_kernel(counts, cols, tiles, node_grad, weight, dense, terms, grad_t):
    def clear(b, carry):
        dense[pl.ds(pl.multiple_of(b * 128, 128), 128), :] = jnp.zeros((128, 2048), BF16)
        return carry

    lax.fori_loop(0, 8, clear, 0)
    start = jnp.int32(0)
    for b in range(8):
        count = counts[b]

        def place(i, carry, b=b, start=start):
            slot = start + i
            col = pl.multiple_of(cols[slot] * 128, 128)
            dense[b * 128 : (b + 1) * 128, pl.ds(col, 128)] = tiles[slot]
            return carry

        lax.fori_loop(0, count, place, 0)
        start = start + count
    grad_t[...] = lax.dot_general(
        weight[...], node_grad[...], (((1,), (1,)), ((), ())), preferred_element_type=F32
    ).astype(BF16)
    for k in range(8):
        term = jnp.dot(
            grad_t[...], dense[:, k * 256 : (k + 1) * 256], preferred_element_type=F32
        )
        terms[k] = term.T.astype(BF16)


def forward_kernel(dense, received, partial):
    total = jnp.zeros((128, 128), F32)
    for k in range(8):
        total = total + jnp.dot(
            dense[:, k * 256 : (k + 1) * 256], received[k, 0:256, :], preferred_element_type=F32
        )
    partial[...] = total.astype(BF16)


def aggregate_kernel(rep, scaling, parts, node_grad, column_sum, message):
    total = parts[0].astype(F32)
    for a in range(1, 16):
        total = total + parts[a].astype(F32)
    piece = total.astype(BF16)
    message[:, 0:64, :] = jnp.broadcast_to(piece[None], (16, 64, 128))
    message[:, 64:80, :] = column_sum[...].reshape(16, 16, 128)
    rows = node_grad[pl.ds(pl.multiple_of(rep[0] * 64, 64), 64), :]
    term = lax.dot_general(piece, rows, (((0,), (0,)), ((), ())), preferred_element_type=F32)
    term = term * scaling
    halves = jnp.concatenate(
        [term[:, 0:128].reshape(16, 8, 128), term[:, 128:256].reshape(16, 8, 128)], axis=1
    )
    high, low = split_high_low(halves)
    message[:, 80:96, :] = high
    message[:, 96:112, :] = low


def output_kernel(received, weight, output, column_piece, weight_part):
    for zq in range(4):
        aggregate = received[zq * 4 : zq * 4 + 4, 0:64, :].reshape(256, 128)
        output[zq * 256 : (zq + 1) * 256, :] = jnp.dot(
            aggregate, weight[...], preferred_element_type=F32
        ).astype(BF16)
    for part in range(4):
        total = received[part, 64:80, :].astype(F32)
        for zh in range(1, 4):
            total = total + received[zh * 4 + part, 64:80, :].astype(F32)
        column_piece[part * 16 : (part + 1) * 16, :] = total.astype(BF16)
    total = received[0, 80:96, :].astype(F32) + received[0, 96:112, :].astype(F32)
    for a in range(1, 16):
        total = total + (received[a, 80:96, :].astype(F32) + received[a, 96:112, :].astype(F32))
    weight_part[...] = total


def exchange(block, axes):
    return lax.all_to_all(block, axes, 0, 0)


def broadcast(block, count, axes):
    return exchange(jnp.broadcast_to(block[None], (count, *block.shape)), axes)


def body(features, tile_values, tile_counts, tile_columns, weight, node_grad):
    tiles = tile_values[0, 0]
    rep_index = lax.axis_index(REP)
    scaling = 1.0 / math.sqrt(features.shape[0] * 32)

    quarter = lax.dynamic_slice_in_dim(features, (rep_index % 4) * 256, 256, axis=0)
    quarter = lax.ppermute(quarter, REP + ROW, PAIRS)

    dense, terms = pl.pallas_call(
        backward_kernel,
        out_shape=(
            jax.ShapeDtypeStruct((1024, 2048), BF16),
            jax.ShapeDtypeStruct((8, 256, 128), BF16),
        ),
        in_specs=[SMEM, SMEM, VMEM, VMEM, VMEM],
        out_specs=(VMEM, VMEM),
        scratch_shapes=[pltpu.VMEM((128, 1024), BF16)],
        compiler_params=PARAMS,
        cost_estimate=pl.CostEstimate(
            flops=2 * 128 * 1024 * 2304, bytes_accessed=8 << 20, transcendentals=0
        ),
        name="backward",
    )(tile_counts[0, 0], tile_columns[0, 0], tiles, node_grad, weight)

    received = exchange(
        jnp.concatenate([jnp.broadcast_to(quarter[None], (8, 256, 128)), terms], axis=1), YC
    )

    column_sum = jnp.sum(received[:, 256:].astype(F32), axis=0).astype(BF16)
    column_sum = lax.ppermute(column_sum, REP + ROW, [(d, s) for s, d in PAIRS])

    partial = pl.pallas_call(
        forward_kernel,
        grid=(8,),
        out_shape=jax.ShapeDtypeStruct((1024, 128), BF16),
        in_specs=[
            pl.BlockSpec((128, 2048), lambda b: (b, 0)),
            pl.BlockSpec((8, 512, 128), lambda b: (0, 0, 0)),
        ],
        out_specs=pl.BlockSpec((128, 128), lambda b: (b, 0)),
        compiler_params=PARAMS,
        cost_estimate=pl.CostEstimate(
            flops=2 * 128 * 1024 * 2048, bytes_accessed=6 << 20, transcendentals=0
        ),
        name="forward",
    )(dense, received)
    parts = exchange(partial.reshape(16, 64, 128), REP)

    message = pl.pallas_call(
        lambda rep, *refs: aggregate_kernel(rep, scaling, *refs),
        out_shape=jax.ShapeDtypeStruct((16, 112, 128), BF16),
        in_specs=[SMEM, VMEM, VMEM, VMEM],
        out_specs=VMEM,
        compiler_params=PARAMS,
        name="aggregate",
    )(rep_index.astype(jnp.int32).reshape(1), parts, node_grad, column_sum)
    received = exchange(message, REP)

    output, column_piece, weight_part = pl.pallas_call(
        output_kernel,
        out_shape=(
            jax.ShapeDtypeStruct((1024, 256), BF16),
            jax.ShapeDtypeStruct((64, 128), BF16),
            jax.ShapeDtypeStruct((16, 128), F32),
        ),
        in_specs=[VMEM, VMEM],
        out_specs=(VMEM, VMEM, VMEM),
        compiler_params=PARAMS,
        name="output",
    )(received, weight)

    weight_part = jnp.sum(broadcast(weight_part, 8, YC), axis=0)
    weight_part = jnp.sum(broadcast(weight_part, 4, ("zh",)), axis=0)
    high, low = split_high_low(weight_part)
    final = broadcast(jnp.concatenate([column_piece, high, low], axis=0), 16, REP)
    feature_grad = (
        final[:, 0:64].reshape(16, 4, 16, 128).transpose(1, 0, 2, 3).reshape(1024, 128)
    )
    weight_grad = final[:, 64:80].astype(F32) + final[:, 80:96].astype(F32)
    weight_grad = (
        weight_grad.reshape(16, 2, 8, 128).transpose(0, 2, 1, 3).reshape(128, 256)
    )
    return output, weight_grad, feature_grad


def solution(mesh):
    fine = Mesh(mesh.devices.reshape(4, 4, 4, 4, 2), REP + ROW)
    placed = (
        P(ROW, None),
        P(REP, ROW, None, None, None),
        P(REP, ROW, None),
        P(REP, ROW, None),
        P(),
        P(ROW, None),
    )
    return jax.shard_map(
        body,
        mesh=fine,
        in_specs=placed,
        out_specs=(P(ROW, None), P(), P(ROW, None)),
        check_vma=False,
    )
```

```python
import math

import jax
import jax.numpy as jnp
from jax import lax
from jax.experimental import pallas as pl
from jax.experimental.pallas import tpu as pltpu
from jax.sharding import Mesh
from jax.sharding import PartitionSpec as P

REP = ("zl", "x")
ROW = ("zh", "y", "c")
YC = ("y", "c")
F32 = jnp.float32
BF16 = jnp.bfloat16
VMEM = pl.BlockSpec(memory_space=pltpu.VMEM)
SMEM = pl.BlockSpec(memory_space=pltpu.SMEM)
PARAMS = pltpu.CompilerParams(vmem_limit_bytes=40 * 1024 * 1024)

PAIRS = [
    ((zh * 4 + k % 4) * 32 + q + 16 * (k // 4), q * 32 + zh * 8 + k)
    for q in range(16)
    for zh in range(4)
    for k in range(8)
]


def split_high_low(value):
    high = value.astype(BF16)
    return high, (value - high.astype(F32)).astype(BF16)


def backward_kernel(counts, cols, tiles, node_grad, weight, dense, terms, grad_t):
    def clear(b, carry):
        dense[pl.ds(pl.multiple_of(b * 128, 128), 128), :] = jnp.zeros((128, 2048), BF16)
        return carry

    lax.fori_loop(0, 8, clear, 0)
    start = jnp.int32(0)
    for b in range(8):
        count = counts[b]

        def place(i, carry, b=b, start=start):
            slot = start + i
            col = pl.multiple_of(cols[slot] * 128, 128)
            dense[b * 128 : (b + 1) * 128, pl.ds(col, 128)] = tiles[slot]
            return carry

        lax.fori_loop(0, count, place, 0)
        start = start + count
    grad_t[...] = lax.dot_general(
        weight[...], node_grad[...], (((1,), (1,)), ((), ())), preferred_element_type=F32
    ).astype(BF16)
    for k in range(8):
        term = jnp.dot(
            grad_t[...], dense[:, k * 256 : (k + 1) * 256], preferred_element_type=F32
        )
        terms[k] = term.T.astype(BF16)


def forward_kernel(scaling, dense, received, node_grad, message, total):
    for k in range(8):
        term = jnp.dot(
            dense[:, k * 256 : (k + 1) * 256], received[k, 0:256, :], preferred_element_type=F32
        )
        if k == 0:
            total[...] = term
        else:
            total[...] += term
    partial = total[...].astype(BF16)
    message[:, 0:64, :] = partial.reshape(16, 64, 128)
    term = lax.dot_general(
        partial, node_grad[...], (((0,), (0,)), ((), ())), preferred_element_type=F32
    )
    term = term * scaling
    message[:, 64:80, :] = jnp.concatenate(
        [term[:, 0:128].reshape(16, 8, 128), term[:, 128:256].reshape(16, 8, 128)], axis=1
    ).astype(BF16)


def aggregate_kernel(parts, piece, weight_part):
    total = parts[0].astype(F32)
    for a in range(1, 16):
        total = total + parts[a].astype(F32)
    piece[...] = total[0:64].astype(BF16)
    weight_part[...] = jnp.broadcast_to(total[64:80][None], (8, 16, 128))


def output_kernel(received, weight, output, column_piece):
    for zq in range(4):
        aggregate = received[zq * 4 : zq * 4 + 4, 0:64, :].reshape(256, 128)
        output[zq * 256 : (zq + 1) * 256, :] = jnp.dot(
            aggregate, weight[...], preferred_element_type=F32
        ).astype(BF16)
    for part in range(4):
        total = received[part, 64:80, :].astype(F32)
        for zh in range(1, 4):
            total = total + received[zh * 4 + part, 64:80, :].astype(F32)
        column_piece[part * 16 : (part + 1) * 16, :] = total.astype(BF16)


def exchange(block, axes):
    return lax.all_to_all(block, axes, 0, 0)


def broadcast(block, count, axes):
    return exchange(jnp.broadcast_to(block[None], (count, *block.shape)), axes)


def body(features, tile_values, tile_counts, tile_columns, weight, node_grad):
    tiles = tile_values[0, 0]
    rep_index = lax.axis_index(REP)
    scaling = 1.0 / math.sqrt(features.shape[0] * 32)

    quarter = lax.dynamic_slice_in_dim(features, (rep_index % 4) * 256, 256, axis=0)
    quarter = lax.ppermute(quarter, REP + ROW, PAIRS)

    dense, terms = pl.pallas_call(
        backward_kernel,
        out_shape=(
            jax.ShapeDtypeStruct((1024, 2048), BF16),
            jax.ShapeDtypeStruct((8, 256, 128), BF16),
        ),
        in_specs=[SMEM, SMEM, VMEM, VMEM, VMEM],
        out_specs=(VMEM, VMEM),
        scratch_shapes=[pltpu.VMEM((128, 1024), BF16)],
        compiler_params=PARAMS,
        cost_estimate=pl.CostEstimate(
            flops=2 * 128 * 1024 * 2304, bytes_accessed=8 << 20, transcendentals=0
        ),
        name="backward",
    )(tile_counts[0, 0], tile_columns[0, 0], tiles, node_grad, weight)

    received = exchange(
        jnp.concatenate([jnp.broadcast_to(quarter[None], (8, 256, 128)), terms], axis=1), YC
    )

    column_sum = jnp.sum(received[:, 256:].astype(F32), axis=0).astype(BF16)
    received, column_sum = lax.optimization_barrier((received, column_sum))
    column_sum = lax.ppermute(column_sum, REP + ROW, [(d, s) for s, d in PAIRS])

    message = pl.pallas_call(
        lambda *refs: forward_kernel(scaling, *refs),
        out_shape=jax.ShapeDtypeStruct((16, 80, 128), BF16),
        in_specs=[VMEM, VMEM, VMEM],
        out_specs=VMEM,
        scratch_shapes=[pltpu.VMEM((1024, 128), F32)],
        compiler_params=PARAMS,
        cost_estimate=pl.CostEstimate(
            flops=2 * 128 * 1024 * 2304, bytes_accessed=6 << 20, transcendentals=0
        ),
        name="forward",
    )(dense, received, node_grad)
    parts = exchange(message, REP)

    piece, weight_part = pl.pallas_call(
        aggregate_kernel,
        out_shape=(
            jax.ShapeDtypeStruct((64, 128), BF16),
            jax.ShapeDtypeStruct((8, 16, 128), F32),
        ),
        in_specs=[VMEM],
        out_specs=(VMEM, VMEM),
        compiler_params=PARAMS,
        name="aggregate",
    )(parts)
    weight_part = jnp.sum(exchange(weight_part, YC), axis=0)
    message = jnp.concatenate(
        [jnp.broadcast_to(piece[None], (16, 64, 128)), column_sum.reshape(16, 16, 128)], axis=1
    )
    message, weight_part = lax.optimization_barrier((message, weight_part))
    others = [
        lax.ppermute(weight_part, "zh", [(i, (i + k) % 4) for i in range(4)]) for k in (1, 2, 3)
    ]
    received = exchange(message, REP)

    output, column_piece = pl.pallas_call(
        output_kernel,
        out_shape=(
            jax.ShapeDtypeStruct((1024, 256), BF16),
            jax.ShapeDtypeStruct((64, 128), BF16),
        ),
        in_specs=[VMEM, VMEM],
        out_specs=(VMEM, VMEM),
        compiler_params=PARAMS,
        name="output",
    )(received, weight)

    weight_part = (weight_part + others[1]) + (others[0] + others[2])
    high, low = split_high_low(weight_part)
    final = broadcast(jnp.concatenate([column_piece, high, low], axis=0), 16, REP)
    feature_grad = (
        final[:, 0:64].reshape(16, 4, 16, 128).transpose(1, 0, 2, 3).reshape(1024, 128)
    )
    weight_grad = final[:, 64:80].astype(F32) + final[:, 80:96].astype(F32)
    weight_grad = (
        weight_grad.reshape(16, 2, 8, 128).transpose(0, 2, 1, 3).reshape(128, 256)
    )
    return output, weight_grad, feature_grad


def solution(mesh):
    fine = Mesh(mesh.devices.reshape(4, 4, 4, 4, 2), REP + ROW)
    placed = (
        P(ROW, None),
        P(REP, ROW, None, None, None),
        P(REP, ROW, None),
        P(REP, ROW, None),
        P(),
        P(ROW, None),
    )
    return jax.shard_map(
        body,
        mesh=fine,
        in_specs=placed,
        out_specs=(P(ROW, None), P(), P(ROW, None)),
        check_vma=False,
    )
```

```python
import math

import jax
import jax.numpy as jnp
from jax import lax
from jax.experimental import pallas as pl
from jax.experimental.pallas import tpu as pltpu
from jax.sharding import Mesh
from jax.sharding import PartitionSpec as P

REP = ("zl", "x")
ROW = ("zh", "y", "c")
F32 = jnp.float32
BF16 = jnp.bfloat16
VMEM = pl.BlockSpec(memory_space=pltpu.VMEM)
SMEM = pl.BlockSpec(memory_space=pltpu.SMEM)
HBM = pl.BlockSpec(memory_space=pltpu.HBM)

PAIRS = [
    ((zh * 4 + k % 4) * 32 + q + 16 * (k // 4), q * 32 + zh * 8 + k)
    for q in range(16)
    for zh in range(4)
    for k in range(8)
]
SWAP = [(0, 1), (1, 0)]


def shape(*dims, dtype=BF16):
    return jax.ShapeDtypeStruct(dims, dtype)


def columns(dense, k):
    return dense[:, pl.ds(pl.multiple_of(k * 256, 256), 256)]


def backward_kernel(
    counts, cols, tiles_hbm, grad_hbm, weight_hbm, dense, terms,
    tiles, node_grad, weight, grad_t, sems,
):
    copies = [
        pltpu.make_async_copy(weight_hbm, weight, sems.at[0]),
        pltpu.make_async_copy(grad_hbm, node_grad, sems.at[1]),
        pltpu.make_async_copy(tiles_hbm, tiles, sems.at[2]),
    ]
    for copy in copies:
        copy.start()

    def clear(b, carry):
        dense[pl.ds(pl.multiple_of(b * 128, 128), 128), :] = jnp.zeros((128, 2048), BF16)
        return carry

    lax.fori_loop(0, 8, clear, 0)
    copies[0].wait()
    copies[1].wait()
    grad_t[...] = lax.dot_general(
        weight[...], node_grad[...], (((1,), (1,)), ((), ())), preferred_element_type=F32
    ).astype(BF16)
    copies[2].wait()
    start = jnp.int32(0)
    for b in range(8):
        count = counts[b]

        def place(i, carry, b=b, start=start):
            slot = start + i
            col = pl.multiple_of(cols[slot] * 128, 128)
            dense[b * 128 : (b + 1) * 128, pl.ds(col, 128)] = tiles[slot]
            return carry

        lax.fori_loop(0, count, place, 0)
        start = start + count
    for k in range(8):
        term = jnp.dot(
            grad_t[...], dense[:, k * 256 : (k + 1) * 256], preferred_element_type=F32
        )
        terms[k % 2, k // 2] = term.T.astype(BF16)


def pack_kernel(terms, quarter, message):
    for y in range(4):
        message[y, 0:256, :] = quarter[...]
        message[y, 256:512, :] = (terms[0, y].astype(F32) + terms[1, y].astype(F32)).astype(BF16)


def split_kernel(received, held, column_sum):
    total = received[0, 256:512, :].astype(F32)
    for y in range(1, 4):
        total = total + received[y, 256:512, :].astype(F32)
    column_sum[...] = total.astype(BF16)
    held[...] = received[:, 0:256, :]


def half_kernel(core, dense, held, total):
    for y in range(4):
        term = jnp.dot(columns(dense, 2 * y + core[0]), held[y], preferred_element_type=F32)
        if y == 0:
            total[...] = term
        else:
            total[...] += term


def forward_kernel(scaling, core, dense, held, half, node_grad, column_sum, message, total):
    for y in range(4):
        term = jnp.dot(columns(dense, 2 * y + 1 - core[0]), held[y], preferred_element_type=F32)
        if y == 0:
            total[...] = half[...] + term
        else:
            total[...] += term
    partial = total[...].astype(BF16)
    message[:, 0:64, :] = partial.reshape(16, 64, 128)
    message[:, 64:80, :] = column_sum[...].reshape(16, 16, 128)
    term = lax.dot_general(
        partial, node_grad[...], (((0,), (0,)), ((), ())), preferred_element_type=F32
    )
    term = term * scaling
    message[:, 80:96, :] = jnp.concatenate(
        [term[:, 0:128].reshape(16, 8, 128), term[:, 128:256].reshape(16, 8, 128)], axis=1
    ).astype(BF16)


def weight_kernel(parts, weight_part):
    total = parts[0, 80:96, :].astype(F32)
    for a in range(1, 16):
        total = total + parts[a, 80:96, :].astype(F32)
    weight_part[...] = total


def reduce_kernel(parts, piece):
    total = parts[0, 0:64, :].astype(F32)
    for a in range(1, 16):
        total = total + parts[a, 0:64, :].astype(F32)
    piece[0:64, :] = total.astype(BF16)
    for part in range(4):
        total = parts[part, 64:80, :].astype(F32)
        for zh in range(1, 4):
            total = total + parts[zh * 4 + part, 64:80, :].astype(F32)
        piece[64 + part * 16 : 80 + part * 16, :] = total.astype(BF16)


def gather_kernel(piece, weight_parts, message):
    message[:, 0:128, :] = jnp.broadcast_to(piece[...][None], (16, 128, 128))
    total = weight_parts[0]
    for i in range(1, 16):
        total = total + weight_parts[i]
    message[:, 128:144, :] = jnp.broadcast_to(total.astype(BF16)[None], (16, 16, 128))


def output_kernel(received, weight, output, weight_grad, feature_grad):
    parts = received[:, 128:144, :].astype(F32)
    weight_grad[:, 0:128] = parts[:, 0:8, :].reshape(128, 128)
    weight_grad[:, 128:256] = parts[:, 8:16, :].reshape(128, 128)
    for zq in range(4):
        aggregate = received[zq * 4 : zq * 4 + 4, 0:64, :].reshape(256, 128)
        output[zq * 256 : (zq + 1) * 256, :] = jnp.dot(
            aggregate, weight[...], preferred_element_type=F32
        ).astype(BF16)
        feature_grad[zq * 256 : (zq + 1) * 256, :] = received[
            :, 64 + zq * 16 : 80 + zq * 16, :
        ].reshape(256, 128)


def call(kernel, name, outs, ins, scratch=(), flops=0, moved=1 << 20, limit=16):
    return pl.pallas_call(
        kernel,
        out_shape=outs,
        in_specs=ins,
        out_specs=jax.tree.map(lambda _: VMEM, outs),
        scratch_shapes=list(scratch),
        compiler_params=pltpu.CompilerParams(vmem_limit_bytes=limit << 20),
        cost_estimate=pl.CostEstimate(flops=flops, bytes_accessed=moved, transcendentals=0),
        name=name,
    )


def exchange(block, axes):
    return lax.all_to_all(block, axes, 0, 0)


def broadcast(block, count, axes):
    return exchange(jnp.broadcast_to(block[None], (count, *block.shape)), axes)


def body(features, tile_values, tile_counts, tile_columns, weight, node_grad):
    rep_index = lax.axis_index(REP)
    core = lax.axis_index("c").astype(jnp.int32).reshape(1)
    scaling = 1.0 / math.sqrt(features.shape[0] * 32)

    quarter = lax.dynamic_slice_in_dim(features, (rep_index % 4) * 256, 256, axis=0)
    quarter = lax.ppermute(quarter, REP + ROW, PAIRS)

    dense, terms = call(
        backward_kernel,
        "backward",
        (shape(1024, 2048), shape(2, 4, 256, 128)),
        [SMEM, SMEM, HBM, HBM, HBM],
        [
            pltpu.VMEM((96, 128, 128), BF16),
            pltpu.VMEM((1024, 256), BF16),
            pltpu.VMEM((128, 256), BF16),
            pltpu.VMEM((128, 1024), BF16),
            pltpu.SemaphoreType.DMA((3,)),
        ],
        flops=2 * 128 * 1024 * 2304,
        moved=8 << 20,
        limit=58,
    )(tile_counts[0, 0], tile_columns[0, 0], tile_values[0, 0], node_grad, weight)
    terms = exchange(terms, "c")
    message = call(pack_kernel, "pack", shape(4, 512, 128), [VMEM] * 2)(terms, quarter)
    received = exchange(message, "y")

    held, column_sum = call(
        split_kernel, "split", (shape(4, 256, 128), shape(256, 128)), [VMEM]
    )(received)
    column_sum = lax.ppermute(column_sum, REP + ROW, [(d, s) for s, d in PAIRS])
    theirs = lax.ppermute(held, "c", SWAP)
    half = call(
        half_kernel,
        "half",
        shape(1024, 128, dtype=F32),
        [SMEM, VMEM, VMEM],
        flops=2 * 128 * 1024 * 1024,
        moved=3 << 20,
    )(core, dense, held)
    message = call(
        lambda *refs: forward_kernel(scaling, *refs),
        "forward",
        shape(16, 96, 128),
        [SMEM] + [VMEM] * 5,
        [pltpu.VMEM((1024, 128), F32)],
        flops=2 * 128 * 1024 * 1280,
        moved=3 << 20,
    )(core, dense, theirs, half, node_grad, column_sum)
    parts = exchange(message, REP)

    weight_part = call(weight_kernel, "weight", shape(16, 128, dtype=F32), [VMEM])(parts)
    weight_other = lax.ppermute(weight_part, "c", SWAP)
    piece = call(reduce_kernel, "reduce", shape(128, 128), [VMEM])(parts)
    weight_parts = broadcast(weight_part + weight_other, 16, ("zh", "y"))
    message = call(gather_kernel, "gather", shape(16, 144, 128), [VMEM] * 2)(piece, weight_parts)
    received = exchange(message, REP)
    return call(
        output_kernel,
        "output",
        (shape(1024, 256), shape(128, 256, dtype=F32), shape(1024, 128)),
        [VMEM, VMEM],
    )(received, weight)


def solution(mesh):
    fine = Mesh(mesh.devices.reshape(4, 4, 4, 4, 2), REP + ROW)
    placed = (
        P(ROW, None),
        P(REP, ROW, None, None, None),
        P(REP, ROW, None),
        P(REP, ROW, None),
        P(),
        P(ROW, None),
    )
    return jax.shard_map(
        body,
        mesh=fine,
        in_specs=placed,
        out_specs=(P(ROW, None), P(), P(ROW, None)),
        check_vma=False,
    )
```

```python
import math

import jax
import jax.numpy as jnp
from jax import lax
from jax.experimental import pallas as pl
from jax.experimental.pallas import tpu as pltpu
from jax.sharding import Mesh
from jax.sharding import PartitionSpec as P

REP = ("zl", "x")
ROW = ("zh", "y", "c")
YC = ("y", "c")
F32 = jnp.float32
BF16 = jnp.bfloat16
VMEM = pl.BlockSpec(memory_space=pltpu.VMEM)
SMEM = pl.BlockSpec(memory_space=pltpu.SMEM)
PARAMS = pltpu.CompilerParams(vmem_limit_bytes=40 * 1024 * 1024)

PAIRS = [
    ((zh * 4 + k % 4) * 32 + q + 16 * (k // 4), q * 32 + zh * 8 + k)
    for q in range(16)
    for zh in range(4)
    for k in range(8)
]


def split_high_low(value):
    high = value.astype(BF16)
    return high, (value - high.astype(F32)).astype(BF16)


def backward_kernel(counts, cols, tiles, node_grad, weight, dense, terms, grad_t):
    def clear(b, carry):
        dense[pl.ds(pl.multiple_of(b * 128, 128), 128), :] = jnp.zeros((128, 2048), BF16)
        return carry

    lax.fori_loop(0, 8, clear, 0)
    start = jnp.int32(0)
    for b in range(8):
        count = counts[b]

        def place(i, carry, b=b, start=start):
            slot = start + i
            col = pl.multiple_of(cols[slot] * 128, 128)
            dense[b * 128 : (b + 1) * 128, pl.ds(col, 128)] = tiles[slot]
            return carry

        lax.fori_loop(0, count, place, 0)
        start = start + count
    grad_t[...] = lax.dot_general(
        weight[...], node_grad[...], (((1,), (1,)), ((), ())), preferred_element_type=F32
    ).astype(BF16)
    for k in range(8):
        term = jnp.dot(
            grad_t[...], dense[:, k * 256 : (k + 1) * 256], preferred_element_type=F32
        )
        terms[k] = term.T.astype(BF16)


def forward_kernel(scaling, dense, quarters, node_grad, message, total):
    for k in range(8):
        term = jnp.dot(
            dense[:, k * 256 : (k + 1) * 256], quarters[k], preferred_element_type=F32
        )
        if k == 0:
            total[...] = term
        else:
            total[...] += term
    partial = total[...].astype(BF16)
    message[:, 0:64, :] = partial.reshape(16, 64, 128)
    term = lax.dot_general(
        partial, node_grad[...], (((0,), (0,)), ((), ())), preferred_element_type=F32
    )
    term = term * scaling
    message[:, 64:80, :] = jnp.concatenate(
        [term[:, 0:128].reshape(16, 8, 128), term[:, 128:256].reshape(16, 8, 128)], axis=1
    ).astype(BF16)


def sum_parts(parts, first, last):
    total = parts[0, first:last, :].astype(F32)
    for i in range(1, parts.shape[0]):
        total = total + parts[i, first:last, :].astype(F32)
    return total


def reduce_kernel(parts, terms, piece, message):
    piece[...] = sum_parts(parts, 0, 64).astype(BF16)
    high, low = split_high_low(sum_parts(parts, 64, 80))
    message[:, 0:256, :] = terms[...]
    message[:, 256:272, :] = jnp.broadcast_to(high[None], (8, 16, 128))
    message[:, 272:288, :] = jnp.broadcast_to(low[None], (8, 16, 128))


def column_kernel(parts, message):
    message[:, 0:64, :] = sum_parts(parts, 0, 256).astype(BF16).reshape(4, 64, 128)
    high, low = split_high_low(sum_parts(parts, 256, 272) + sum_parts(parts, 272, 288))
    message[:, 64:80, :] = jnp.broadcast_to(high[None], (4, 16, 128))
    message[:, 80:96, :] = jnp.broadcast_to(low[None], (4, 16, 128))


def column_sum_kernel(parts, column_piece):
    column_piece[...] = sum_parts(parts, 0, 64).astype(BF16)


def gather_kernel(piece, column_piece, parts, message):
    weight_part = (sum_parts(parts, 64, 80) + sum_parts(parts, 80, 96)).astype(BF16)
    message[:, 0:64, :] = jnp.broadcast_to(piece[...][None], (16, 64, 128))
    message[:, 64:128, :] = jnp.broadcast_to(column_piece[...][None], (16, 64, 128))
    message[:, 128:144, :] = jnp.broadcast_to(weight_part[None], (16, 16, 128))


def output_kernel(received, weight, output, weight_grad, feature_grad):
    parts = received[:, 128:144, :].astype(F32)
    weight_grad[:, 0:128] = parts[:, 0:8, :].reshape(128, 128)
    weight_grad[:, 128:256] = parts[:, 8:16, :].reshape(128, 128)
    for a in range(16):
        row = a % 4 * 256 + a // 4 * 64
        feature_grad[row : row + 64, :] = received[a, 64:128, :]
    for quarter in range(4):
        aggregate = received[quarter * 4 : quarter * 4 + 4, 0:64, :].reshape(256, 128)
        output[quarter * 256 : (quarter + 1) * 256, :] = jnp.dot(
            aggregate, weight[...], preferred_element_type=F32
        ).astype(BF16)


def shape(*dims, dtype=BF16):
    return jax.ShapeDtypeStruct(dims, dtype)


def call(kernel, name, outs, ins, scratch=(), flops=0, moved=1 << 20):
    return pl.pallas_call(
        kernel,
        out_shape=outs,
        in_specs=ins,
        out_specs=jax.tree.map(lambda _: VMEM, outs),
        scratch_shapes=list(scratch),
        compiler_params=PARAMS,
        cost_estimate=pl.CostEstimate(flops=flops, bytes_accessed=moved, transcendentals=0),
        name=name,
    )


def exchange(block, axes):
    return lax.all_to_all(block, axes, 0, 0)


def body(features, tile_values, tile_counts, tile_columns, weight, node_grad):
    rep_index = lax.axis_index(REP)
    scaling = 1.0 / math.sqrt(features.shape[0] * 32)

    quarter = lax.dynamic_slice_in_dim(features, (rep_index % 4) * 256, 256, axis=0)
    quarter = lax.ppermute(quarter, REP + ROW, PAIRS)
    dense, terms = call(
        backward_kernel,
        "backward",
        (shape(1024, 2048), shape(8, 256, 128)),
        [SMEM, SMEM, VMEM, VMEM, VMEM],
        [pltpu.VMEM((128, 1024), BF16)],
        flops=2 * 128 * 1024 * 2304,
        moved=8 << 20,
    )(tile_counts[0, 0], tile_columns[0, 0], tile_values[0, 0], node_grad, weight)

    quarter, terms = lax.optimization_barrier((quarter, terms))
    quarters = exchange(jnp.broadcast_to(quarter[None], (8, 256, 128)), YC)
    message = call(
        lambda *refs: forward_kernel(scaling, *refs),
        "forward",
        shape(16, 80, 128),
        [VMEM] * 3,
        [pltpu.VMEM((1024, 128), F32)],
        flops=2 * 128 * 1024 * 2304,
        moved=6 << 20,
    )(dense, quarters, node_grad)
    parts = exchange(message, REP)

    piece, message = call(
        reduce_kernel, "reduce", (shape(64, 128), shape(8, 288, 128)), [VMEM] * 2
    )(parts, terms)
    parts = exchange(message, YC)
    message = call(column_kernel, "column", shape(4, 96, 128), [VMEM])(parts)
    parts = exchange(message, "zh")
    column_piece = call(column_sum_kernel, "column_sum", shape(64, 128), [VMEM])(parts)
    column_piece = lax.ppermute(column_piece, REP + ROW, [(d, s) for s, d in PAIRS])
    message = call(gather_kernel, "gather", shape(16, 144, 128), [VMEM] * 3)(
        piece, column_piece, parts
    )
    received = exchange(message, REP)
    return call(
        output_kernel,
        "output",
        (shape(1024, 256), shape(128, 256, dtype=F32), shape(1024, 128)),
        [VMEM] * 2,
    )(received, weight)


def solution(mesh):
    fine = Mesh(mesh.devices.reshape(4, 4, 4, 4, 2), REP + ROW)
    placed = (
        P(ROW, None),
        P(REP, ROW, None, None, None),
        P(REP, ROW, None),
        P(REP, ROW, None),
        P(),
        P(ROW, None),
    )
    return jax.shard_map(
        body,
        mesh=fine,
        in_specs=placed,
        out_specs=(P(ROW, None), P(), P(ROW, None)),
        check_vma=False,
    )
```

```python
import math

import jax
import jax.numpy as jnp
from jax import lax
from jax.experimental import pallas as pl
from jax.experimental.pallas import tpu as pltpu
from jax.sharding import Mesh
from jax.sharding import PartitionSpec as P

REP = ("zl", "x")
ROW = ("zh", "y", "c")
F32 = jnp.float32
BF16 = jnp.bfloat16
VMEM = pl.BlockSpec(memory_space=pltpu.VMEM)
SMEM = pl.BlockSpec(memory_space=pltpu.SMEM)
HBM = pl.BlockSpec(memory_space=pltpu.HBM)

NEAR = ((1, 2, 3, 0), (2, 3, 0, 1))


def pair(q, zh, k):
    home = k // 4 * 2 + q // 8
    a = NEAR[q // 8][(zh - home) % 4] * 4 + k % 4
    return a * 32 + q + k // 4 * 16, q * 32 + zh * 8 + k


PAIRS = [pair(q, zh, k) for q in range(16) for zh in range(4) for k in range(8)]
SWAP = [(0, 1), (1, 0)]


def shape(*dims, dtype=BF16):
    return jax.ShapeDtypeStruct(dims, dtype)


def columns(dense, k):
    return dense[:, pl.ds(pl.multiple_of(k * 256, 256), 256)]


def fill(counts, cols, tiles, dense):
    def clear(b, carry):
        dense[pl.ds(pl.multiple_of(b * 128, 128), 128), :] = jnp.zeros((128, 2048), BF16)
        return carry

    lax.fori_loop(0, 8, clear, 0)
    yield
    start = jnp.int32(0)
    for b in range(8):
        count = counts[b]

        def place(i, carry, b=b, start=start):
            slot = start + i
            col = pl.multiple_of(cols[slot] * 128, 128)
            dense[b * 128 : (b + 1) * 128, pl.ds(col, 128)] = tiles[slot]
            return carry

        lax.fori_loop(0, count, place, 0)
        start = start + count
    yield


def backward_kernel(
    counts, cols, tiles_hbm, grad_hbm, weight_hbm, terms,
    tiles, node_grad, weight, dense, grad_t, sems,
):
    copies = [
        pltpu.make_async_copy(weight_hbm, weight, sems.at[0]),
        pltpu.make_async_copy(grad_hbm, node_grad, sems.at[1]),
        pltpu.make_async_copy(tiles_hbm, tiles, sems.at[2]),
    ]
    for copy in copies:
        copy.start()
    filling = fill(counts, cols, tiles, dense)
    next(filling)
    copies[0].wait()
    copies[1].wait()
    grad_t[...] = lax.dot_general(
        weight[...], node_grad[...], (((1,), (1,)), ((), ())), preferred_element_type=F32
    ).astype(BF16)
    copies[2].wait()
    next(filling)
    for k in range(8):
        term = jnp.dot(
            grad_t[...], dense[:, k * 256 : (k + 1) * 256], preferred_element_type=F32
        )
        terms[k % 2, k // 2] = term.T.astype(BF16)


def pack_kernel(terms, quarter, message):
    for y in range(4):
        message[y, 0:256, :] = quarter[...]
        message[y, 256:512, :] = (terms[0, y].astype(F32) + terms[1, y].astype(F32)).astype(BF16)


def split_kernel(received, held, column_sum):
    total = received[0, 256:512, :].astype(F32)
    for y in range(1, 4):
        total = total + received[y, 256:512, :].astype(F32)
    column_sum[...] = total.astype(BF16)
    held[...] = received[:, 0:256, :]


def half_kernel(core, counts, cols, tiles, held, dense, total):
    for _ in fill(counts, cols, tiles, dense):
        pass
    for y in range(4):
        term = jnp.dot(columns(dense, 2 * y + core[0]), held[y], preferred_element_type=F32)
        if y == 0:
            total[...] = term
        else:
            total[...] += term


def forward_kernel(scaling, core, dense, held, half, node_grad, column_sum, message, total):
    for y in range(4):
        term = jnp.dot(columns(dense, 2 * y + 1 - core[0]), held[y], preferred_element_type=F32)
        if y == 0:
            total[...] = half[...] + term
        else:
            total[...] += term
    partial = total[...].astype(BF16)
    message[:, 0:64, :] = partial.reshape(16, 64, 128)
    message[:, 64:80, :] = column_sum[...].reshape(16, 16, 128)
    term = lax.dot_general(
        partial, node_grad[...], (((0,), (0,)), ((), ())), preferred_element_type=F32
    )
    term = term * scaling
    message[:, 80:96, :] = jnp.concatenate(
        [term[:, 0:128].reshape(16, 8, 128), term[:, 128:256].reshape(16, 8, 128)], axis=1
    ).astype(BF16)


def reduce_kernel(parts, piece, weight_part):
    total = parts[0, 0:64, :].astype(F32)
    for a in range(1, 16):
        total = total + parts[a, 0:64, :].astype(F32)
    piece[0:64, :] = total.astype(BF16)
    for part in range(4):
        total = parts[part, 64:80, :].astype(F32)
        for zl in range(1, 4):
            total = total + parts[zl * 4 + part, 64:80, :].astype(F32)
        piece[64 + part * 16 : 80 + part * 16, :] = total.astype(BF16)
    total = parts[0, 80:96, :].astype(F32)
    for a in range(1, 16):
        total = total + parts[a, 80:96, :].astype(F32)
    weight_part[...] = jnp.broadcast_to(total.astype(BF16)[None], (32, 16, 128))


def gather_kernel(piece, weight_parts, message):
    message[:, 0:128, :] = jnp.broadcast_to(piece[...][None], (16, 128, 128))
    total = weight_parts[0].astype(F32)
    for r in range(1, 32):
        total = total + weight_parts[r].astype(F32)
    message[:, 128:144, :] = jnp.broadcast_to(total.astype(BF16)[None], (16, 16, 128))


def output_kernel(received, weight, output, weight_grad, feature_grad):
    parts = received[:, 128:144, :].astype(F32)
    weight_grad[:, 0:128] = parts[:, 0:8, :].reshape(128, 128)
    weight_grad[:, 128:256] = parts[:, 8:16, :].reshape(128, 128)
    for zq in range(4):
        aggregate = received[zq * 4 : zq * 4 + 4, 0:64, :].reshape(256, 128)
        output[zq * 256 : (zq + 1) * 256, :] = jnp.dot(
            aggregate, weight[...], preferred_element_type=F32
        ).astype(BF16)
        feature_grad[zq * 256 : (zq + 1) * 256, :] = received[
            :, 64 + zq * 16 : 80 + zq * 16, :
        ].reshape(256, 128)


def call(kernel, name, outs, ins, scratch=(), flops=0, moved=1 << 20, limit=16):
    return pl.pallas_call(
        kernel,
        out_shape=outs,
        in_specs=ins,
        out_specs=jax.tree.map(lambda _: VMEM, outs),
        scratch_shapes=list(scratch),
        compiler_params=pltpu.CompilerParams(vmem_limit_bytes=limit << 20),
        cost_estimate=pl.CostEstimate(flops=flops, bytes_accessed=moved, transcendentals=0),
        name=name,
    )


def exchange(block, axes):
    return lax.all_to_all(block, axes, 0, 0)


def body(features, tile_values, tile_counts, tile_columns, weight, node_grad):
    rep_index = lax.axis_index(REP)
    core = lax.axis_index("c").astype(jnp.int32).reshape(1)
    scaling = 1.0 / math.sqrt(features.shape[0] * 32)

    quarter = lax.dynamic_slice_in_dim(features, (rep_index % 4) * 256, 256, axis=0)
    quarter = lax.ppermute(quarter, REP + ROW, PAIRS)

    counts, cols, tiles = tile_counts[0, 0], tile_columns[0, 0], tile_values[0, 0]
    terms = call(
        backward_kernel,
        "backward",
        shape(2, 4, 256, 128),
        [SMEM, SMEM, HBM, HBM, HBM],
        [
            pltpu.VMEM((96, 128, 128), BF16),
            pltpu.VMEM((1024, 256), BF16),
            pltpu.VMEM((128, 256), BF16),
            pltpu.VMEM((1024, 2048), BF16),
            pltpu.VMEM((128, 1024), BF16),
            pltpu.SemaphoreType.DMA((3,)),
        ],
        flops=2 * 128 * 1024 * 2304,
        moved=8 << 20,
        limit=58,
    )(counts, cols, tiles, node_grad, weight)
    terms = exchange(terms, "c")
    message = call(pack_kernel, "pack", shape(4, 512, 128), [VMEM] * 2)(terms, quarter)
    received = exchange(message, "y")

    held, column_sum = call(
        split_kernel, "split", (shape(4, 256, 128), shape(256, 128)), [VMEM]
    )(received)
    column_sum = lax.ppermute(column_sum, REP + ROW, [(d, s) for s, d in PAIRS])
    theirs = lax.ppermute(held, "c", SWAP)
    dense, half = call(
        half_kernel,
        "half",
        (shape(1024, 2048), shape(1024, 128, dtype=F32)),
        [SMEM, SMEM, SMEM, VMEM, VMEM],
        flops=2 * 128 * 1024 * 1024,
        moved=3 << 20,
    )(core, counts, cols, tiles, held)
    message = call(
        lambda *refs: forward_kernel(scaling, *refs),
        "forward",
        shape(16, 96, 128),
        [SMEM] + [VMEM] * 5,
        [pltpu.VMEM((1024, 128), F32)],
        flops=2 * 128 * 1024 * 1280,
        moved=3 << 20,
    )(core, dense, theirs, half, node_grad, column_sum)
    parts = exchange(message, REP)

    piece, weight_part = call(
        reduce_kernel, "reduce", (shape(128, 128), shape(32, 16, 128)), [VMEM]
    )(parts)
    weight_parts = exchange(weight_part, ROW)
    message = call(gather_kernel, "gather", shape(16, 144, 128), [VMEM] * 2)(piece, weight_parts)
    received = exchange(message, REP)
    return call(
        output_kernel,
        "output",
        (shape(1024, 256), shape(128, 256, dtype=F32), shape(1024, 128)),
        [VMEM, VMEM],
    )(received, weight)


def solution(mesh):
    fine = Mesh(mesh.devices.reshape(4, 4, 4, 4, 2), REP + ROW)
    placed = (
        P(ROW, None),
        P(REP, ROW, None, None, None),
        P(REP, ROW, None),
        P(REP, ROW, None),
        P(),
        P(ROW, None),
    )
    return jax.shard_map(
        body,
        mesh=fine,
        in_specs=placed,
        out_specs=(P(ROW, None), P(), P(ROW, None)),
        check_vma=False,
    )
```

```python
import math

import jax
import jax.numpy as jnp
from jax import lax
from jax.experimental import pallas as pl
from jax.experimental.pallas import tpu as pltpu
from jax.sharding import Mesh
from jax.sharding import PartitionSpec as P

REP = ("zl", "x")
ROW = ("zh", "y", "c")
F32 = jnp.float32
BF16 = jnp.bfloat16
VMEM = pl.BlockSpec(memory_space=pltpu.VMEM)
SMEM = pl.BlockSpec(memory_space=pltpu.SMEM)
HBM = pl.BlockSpec(memory_space=pltpu.HBM)

NEAR = ((1, 2, 3, 0), (2, 3, 0, 1))


def farther(q, half):
    return 1 - (((q >> 1) + 1) >> 1 & 1) ^ half


def pair(q, zh, k):
    half, turn = k // 4, k % 2
    if k // 2 % 2 != farther(q, half):
        turn += 2
    a = NEAR[q // 8][(zh - half * 2 - q // 8) % 4] * 4 + (q + turn) % 4
    return a * 32 + q + half * 16, q * 32 + zh * 8 + k


def quarter_of(a, s):
    turn = (a - s) % 4
    far = farther(s % 16, s // 16)
    return jnp.where(turn < 2, far, 1 - far) * 2 + turn % 2


PAIRS = [pair(q, zh, k) for q in range(16) for zh in range(4) for k in range(8)]


def shape(*dims, dtype=BF16):
    return jax.ShapeDtypeStruct(dims, dtype)


def fill(counts, cols, tiles, dense):
    def clear(b, carry):
        dense[pl.ds(pl.multiple_of(b * 128, 128), 128), :] = jnp.zeros((128, 2048), BF16)
        return carry

    lax.fori_loop(0, 8, clear, 0)
    yield
    start = jnp.int32(0)
    for b in range(8):
        count = counts[b]

        def place(i, carry, b=b, start=start):
            slot = start + i
            col = pl.multiple_of(cols[slot] * 128, 128)
            dense[b * 128 : (b + 1) * 128, pl.ds(col, 128)] = tiles[slot]
            return carry

        lax.fori_loop(0, count, place, 0)
        start = start + count
    yield


def backward_kernel(
    counts, cols, tiles_hbm, grad_hbm, weight_hbm, terms,
    tiles, node_grad, weight, dense, grad_t, sems,
):
    copies = [
        pltpu.make_async_copy(weight_hbm, weight, sems.at[0]),
        pltpu.make_async_copy(grad_hbm, node_grad, sems.at[1]),
        pltpu.make_async_copy(tiles_hbm, tiles, sems.at[2]),
    ]
    for copy in copies:
        copy.start()
    filling = fill(counts, cols, tiles, dense)
    next(filling)
    copies[0].wait()
    copies[1].wait()
    grad_t[...] = lax.dot_general(
        weight[...], node_grad[...], (((1,), (1,)), ((), ())), preferred_element_type=F32
    ).astype(BF16)
    copies[2].wait()
    next(filling)
    for k in range(8):
        term = jnp.dot(
            grad_t[...], dense[:, k * 256 : (k + 1) * 256], preferred_element_type=F32
        )
        terms[k % 2, k // 2] = term.T.astype(BF16)


def pack_kernel(terms, quarter, message):
    for y in range(4):
        message[y, 0:256, :] = quarter[...]
        message[y, 256:512, :] = (terms[0, y].astype(F32) + terms[1, y].astype(F32)).astype(BF16)


def split_kernel(received, held, column_sum):
    total = received[0, 256:512, :].astype(F32)
    for y in range(1, 4):
        total = total + received[y, 256:512, :].astype(F32)
    column_sum[...] = total.astype(BF16)
    for c in range(2):
        held[c] = received[:, 0:256, :]


def dense_kernel(counts, cols, tiles, dense):
    for _ in fill(counts, cols, tiles, dense):
        pass


def forward_kernel(scaling, dense, held, node_grad, message, total):
    for k in range(8):
        term = jnp.dot(
            dense[:, k * 256 : (k + 1) * 256], held[k % 2, k // 2], preferred_element_type=F32
        )
        if k == 0:
            total[...] = term
        else:
            total[...] += term
    partial = total[...].astype(BF16)
    message[:, 0:64, :] = partial.reshape(16, 64, 128)
    term = lax.dot_general(
        partial, node_grad[...], (((0,), (0,)), ((), ())), preferred_element_type=F32
    )
    term = term * scaling
    message[:, 64:80, :] = jnp.concatenate(
        [term[:, 0:128].reshape(16, 8, 128), term[:, 128:256].reshape(16, 8, 128)], axis=1
    ).astype(BF16)


def reduce_kernel(parts, piece, weight_part):
    total = parts[0, 0:64, :].astype(F32)
    for a in range(1, 16):
        total = total + parts[a, 0:64, :].astype(F32)
    piece[0:64, :] = total.astype(BF16)
    for part in range(4):
        total = parts[part, 80:96, :].astype(F32)
        for zl in range(1, 4):
            total = total + parts[zl * 4 + part, 80:96, :].astype(F32)
        piece[64 + part * 16 : 80 + part * 16, :] = total.astype(BF16)
    total = parts[0, 64:80, :].astype(F32)
    for a in range(1, 16):
        total = total + parts[a, 64:80, :].astype(F32)
    weight_part[...] = jnp.broadcast_to(total.astype(BF16)[None], (32, 16, 128))


def gather_kernel(piece, weight_parts, message):
    message[:, 0:128, :] = jnp.broadcast_to(piece[...][None], (16, 128, 128))
    total = weight_parts[0].astype(F32)
    for r in range(1, 32):
        total = total + weight_parts[r].astype(F32)
    message[:, 128:144, :] = jnp.broadcast_to(total.astype(BF16)[None], (16, 16, 128))


def output_kernel(order, received, weight, output, weight_grad, feature_grad):
    parts = received[:, 128:144, :].astype(F32)
    weight_grad[:, 0:128] = parts[:, 0:8, :].reshape(128, 128)
    weight_grad[:, 128:256] = parts[:, 8:16, :].reshape(128, 128)
    for zq in range(4):
        aggregate = received[zq * 4 : zq * 4 + 4, 0:64, :].reshape(256, 128)
        output[zq * 256 : (zq + 1) * 256, :] = jnp.dot(
            aggregate, weight[...], preferred_element_type=F32
        ).astype(BF16)
        row = pl.multiple_of(order[zq] * 256, 256)
        feature_grad[pl.ds(row, 256), :] = received[
            :, 64 + zq * 16 : 80 + zq * 16, :
        ].reshape(256, 128)


def call(kernel, name, outs, ins, scratch=(), flops=0, moved=1 << 20, limit=16):
    return pl.pallas_call(
        kernel,
        out_shape=outs,
        in_specs=ins,
        out_specs=jax.tree.map(lambda _: VMEM, outs),
        scratch_shapes=list(scratch),
        compiler_params=pltpu.CompilerParams(vmem_limit_bytes=limit << 20),
        cost_estimate=pl.CostEstimate(flops=flops, bytes_accessed=moved, transcendentals=0),
        name=name,
    )


def exchange(block, axes):
    return lax.all_to_all(block, axes, 0, 0)


def body(features, tile_values, tile_counts, tile_columns, weight, node_grad):
    rep_index = lax.axis_index(REP)
    row_index = lax.axis_index(ROW)
    scaling = 1.0 / math.sqrt(features.shape[0] * 32)
    counts, cols, tiles = tile_counts[0, 0], tile_columns[0, 0], tile_values[0, 0]
    order = quarter_of(jnp.arange(4, dtype=jnp.int32), row_index).astype(jnp.int32)

    terms = call(
        backward_kernel,
        "backward",
        shape(2, 4, 256, 128),
        [SMEM, SMEM, HBM, HBM, HBM],
        [
            pltpu.VMEM((96, 128, 128), BF16),
            pltpu.VMEM((1024, 256), BF16),
            pltpu.VMEM((128, 256), BF16),
            pltpu.VMEM((1024, 2048), BF16),
            pltpu.VMEM((128, 1024), BF16),
            pltpu.SemaphoreType.DMA((3,)),
        ],
        flops=2 * 128 * 1024 * 2304,
        moved=8 << 20,
        limit=58,
    )(counts, cols, tiles, node_grad, weight)
    start = quarter_of(rep_index, row_index) * 256
    quarter = lax.dynamic_slice_in_dim(features, start, 256, axis=0)
    quarter, terms = lax.optimization_barrier((quarter, terms))
    quarter = lax.ppermute(quarter, REP + ROW, PAIRS)
    terms = exchange(terms, "c")
    message = call(pack_kernel, "pack", shape(4, 512, 128), [VMEM] * 2)(terms, quarter)
    received = exchange(message, "y")

    held, column_sum = call(
        split_kernel, "split", (shape(2, 4, 256, 128), shape(256, 128)), [VMEM]
    )(received)
    column_sum = lax.ppermute(column_sum, REP + ROW, [(d, s) for s, d in PAIRS])
    dense = call(dense_kernel, "dense", shape(1024, 2048), [SMEM, SMEM, VMEM])(
        counts, cols, tiles
    )
    held, dense = lax.optimization_barrier((held, dense))
    held = exchange(held, "c")
    message = call(
        lambda *refs: forward_kernel(scaling, *refs),
        "forward",
        shape(16, 80, 128),
        [VMEM] * 3,
        [pltpu.VMEM((1024, 128), F32)],
        flops=2 * 128 * 1024 * 2304,
        moved=3 << 20,
    )(dense, held, node_grad)
    message = jnp.concatenate([message, column_sum.reshape(16, 16, 128)], axis=1)
    parts = exchange(message, REP)

    piece, weight_part = call(
        reduce_kernel, "reduce", (shape(128, 128), shape(32, 16, 128)), [VMEM]
    )(parts)
    weight_parts = exchange(weight_part, ROW)
    message = call(gather_kernel, "gather", shape(16, 144, 128), [VMEM] * 2)(piece, weight_parts)
    received = exchange(message, REP)
    return call(
        output_kernel,
        "output",
        (shape(1024, 256), shape(128, 256, dtype=F32), shape(1024, 128)),
        [SMEM, VMEM, VMEM],
    )(order, received, weight)


def solution(mesh):
    fine = Mesh(mesh.devices.reshape(4, 4, 4, 4, 2), REP + ROW)
    placed = (
        P(ROW, None),
        P(REP, ROW, None, None, None),
        P(REP, ROW, None),
        P(REP, ROW, None),
        P(),
        P(ROW, None),
    )
    return jax.shard_map(
        body,
        mesh=fine,
        in_specs=placed,
        out_specs=(P(ROW, None), P(), P(ROW, None)),
        check_vma=False,
    )
```

```python
import math

import jax
import jax.numpy as jnp
from jax import lax
from jax.experimental import pallas as pl
from jax.experimental.pallas import tpu as pltpu
from jax.sharding import Mesh
from jax.sharding import PartitionSpec as P

REP = ("zl", "x")
ROW = ("zh", "y", "c")
F32 = jnp.float32
BF16 = jnp.bfloat16
VMEM = pl.BlockSpec(memory_space=pltpu.VMEM)
SMEM = pl.BlockSpec(memory_space=pltpu.SMEM)
HBM = pl.BlockSpec(memory_space=pltpu.HBM)

NEAR = ((1, 2, 3, 0), (2, 3, 0, 1))


def farther(q, half):
    return 1 - (((q >> 1) + 1) >> 1 & 1) ^ half


def pair(q, zh, k):
    half, turn = k // 4, k % 2
    if k // 2 % 2 != farther(q, half):
        turn += 2
    a = NEAR[q // 8][(zh - half * 2 - q // 8) % 4] * 4 + (q + turn) % 4
    return a * 32 + q + half * 16, q * 32 + zh * 8 + k


def quarter_of(a, s):
    turn = (a - s) % 4
    far = farther(s % 16, s // 16)
    return jnp.where(turn < 2, far, 1 - far) * 2 + turn % 2


PAIRS = [pair(q, zh, k) for q in range(16) for zh in range(4) for k in range(8)]


def shape(*dims, dtype=BF16):
    return jax.ShapeDtypeStruct(dims, dtype)


def fill(counts, cols, tiles, dense):
    def clear(b, carry):
        dense[pl.ds(pl.multiple_of(b * 128, 128), 128), :] = jnp.zeros((128, 2048), BF16)
        return carry

    lax.fori_loop(0, 8, clear, 0)
    yield
    start = jnp.int32(0)
    for b in range(8):
        count = counts[b]

        def place(i, carry, b=b, start=start):
            slot = start + i
            col = pl.multiple_of(cols[slot] * 128, 128)
            dense[b * 128 : (b + 1) * 128, pl.ds(col, 128)] = tiles[slot]
            return carry

        lax.fori_loop(0, count, place, 0)
        start = start + count
    yield


def tile_copies(tiles_hbm, tiles, sems):
    return [
        pltpu.make_async_copy(
            tiles_hbm.at[pl.ds(i * 12, 12)], tiles.at[pl.ds(i * 12, 12)], sems.at[i]
        )
        for i in range(8)
    ]


def backward_kernel(
    counts, cols, tiles_hbm, grad_hbm, weight_hbm, terms,
    tiles, node_grad, weight, dense, grad_t, sems,
):
    copies = [
        pltpu.make_async_copy(weight_hbm, weight, sems.at[8]),
        pltpu.make_async_copy(grad_hbm, node_grad, sems.at[9]),
    ]
    loads = tile_copies(tiles_hbm, tiles, sems)
    for copy in copies + loads:
        copy.start()
    filling = fill(counts, cols, tiles, dense)
    next(filling)
    copies[0].wait()
    copies[1].wait()
    grad_t[...] = lax.dot_general(
        weight[...], node_grad[...], (((1,), (1,)), ((), ())), preferred_element_type=F32
    ).astype(BF16)
    for copy in loads:
        copy.wait()
    next(filling)
    for k in range(8):
        term = jnp.dot(
            grad_t[...], dense[:, k * 256 : (k + 1) * 256], preferred_element_type=F32
        )
        terms[k % 2, k // 2] = term.T.astype(BF16)


def pack_kernel(terms, quarter, message):
    for y in range(4):
        message[y, 0:256, :] = quarter[...]
        message[y, 256:512, :] = (terms[0, y].astype(F32) + terms[1, y].astype(F32)).astype(BF16)


def split_kernel(received, held, column_sum):
    total = received[0, 256:512, :].astype(F32)
    for y in range(1, 4):
        total = total + received[y, 256:512, :].astype(F32)
    column_sum[...] = total.astype(BF16)
    for c in range(2):
        held[c] = received[:, 0:256, :]


def dense_kernel(counts, cols, tiles, dense):
    for _ in fill(counts, cols, tiles, dense):
        pass


def forward_kernel(scaling, dense, held, node_grad, message, total):
    for k in range(8):
        term = jnp.dot(
            dense[:, k * 256 : (k + 1) * 256], held[k % 2, k // 2], preferred_element_type=F32
        )
        if k == 0:
            total[...] = term
        else:
            total[...] += term
    partial = total[...].astype(BF16)
    message[:, 0:64, :] = partial.reshape(16, 64, 128)
    term = lax.dot_general(
        partial, node_grad[...], (((0,), (0,)), ((), ())), preferred_element_type=F32
    )
    term = term * scaling
    message[:, 64:80, :] = jnp.concatenate(
        [term[:, 0:128].reshape(16, 8, 128), term[:, 128:256].reshape(16, 8, 128)], axis=1
    ).astype(BF16)


def reduce_kernel(parts, piece, weight_part):
    total = parts[0, 0:64, :].astype(F32)
    for a in range(1, 16):
        total = total + parts[a, 0:64, :].astype(F32)
    piece[0:64, :] = total.astype(BF16)
    for part in range(4):
        total = parts[part, 80:96, :].astype(F32)
        for zl in range(1, 4):
            total = total + parts[zl * 4 + part, 80:96, :].astype(F32)
        piece[64 + part * 16 : 80 + part * 16, :] = total.astype(BF16)
    total = parts[0, 64:80, :].astype(F32)
    for a in range(1, 16):
        total = total + parts[a, 64:80, :].astype(F32)
    weight_part[...] = jnp.broadcast_to(total.astype(BF16)[None], (32, 16, 128))


def gather_kernel(piece, weight_parts, message):
    message[:, 0:128, :] = jnp.broadcast_to(piece[...][None], (16, 128, 128))
    total = weight_parts[0].astype(F32)
    for r in range(1, 32):
        total = total + weight_parts[r].astype(F32)
    message[:, 128:144, :] = jnp.broadcast_to(total.astype(BF16)[None], (16, 16, 128))


def output_kernel(order, received, weight, output, weight_grad, feature_grad):
    parts = received[:, 128:144, :].astype(F32)
    weight_grad[:, 0:128] = parts[:, 0:8, :].reshape(128, 128)
    weight_grad[:, 128:256] = parts[:, 8:16, :].reshape(128, 128)
    for zq in range(4):
        aggregate = received[zq * 4 : zq * 4 + 4, 0:64, :].reshape(256, 128)
        output[zq * 256 : (zq + 1) * 256, :] = jnp.dot(
            aggregate, weight[...], preferred_element_type=F32
        ).astype(BF16)
        row = pl.multiple_of(order[zq] * 256, 256)
        feature_grad[pl.ds(row, 256), :] = received[
            :, 64 + zq * 16 : 80 + zq * 16, :
        ].reshape(256, 128)


def call(kernel, name, outs, ins, scratch=(), flops=0, moved=1 << 20, limit=16):
    return pl.pallas_call(
        kernel,
        out_shape=outs,
        in_specs=ins,
        out_specs=jax.tree.map(lambda _: VMEM, outs),
        scratch_shapes=list(scratch),
        compiler_params=pltpu.CompilerParams(vmem_limit_bytes=limit << 20),
        cost_estimate=pl.CostEstimate(flops=flops, bytes_accessed=moved, transcendentals=0),
        name=name,
    )


def exchange(block, axes):
    return lax.all_to_all(block, axes, 0, 0)


def body(features, tile_values, tile_counts, tile_columns, weight, node_grad):
    rep_index = lax.axis_index(REP)
    row_index = lax.axis_index(ROW)
    scaling = 1.0 / math.sqrt(features.shape[0] * 32)
    counts, cols, tiles = tile_counts[0, 0], tile_columns[0, 0], tile_values[0, 0]
    order = quarter_of(jnp.arange(4, dtype=jnp.int32), row_index).astype(jnp.int32)

    terms = call(
        backward_kernel,
        "backward",
        shape(2, 4, 256, 128),
        [SMEM, SMEM, HBM, HBM, HBM],
        [
            pltpu.VMEM((96, 128, 128), BF16),
            pltpu.VMEM((1024, 256), BF16),
            pltpu.VMEM((128, 256), BF16),
            pltpu.VMEM((1024, 2048), BF16),
            pltpu.VMEM((128, 1024), BF16),
            pltpu.SemaphoreType.DMA((10,)),
        ],
        flops=2 * 128 * 1024 * 2304,
        moved=8 << 20,
        limit=58,
    )(counts, cols, tiles, node_grad, weight)
    start = quarter_of(rep_index, row_index) * 256
    quarter = lax.dynamic_slice_in_dim(features, start, 256, axis=0)
    quarter = lax.ppermute(quarter, REP + ROW, PAIRS)
    terms = exchange(terms, "c")
    message = call(pack_kernel, "pack", shape(4, 512, 128), [VMEM] * 2)(terms, quarter)
    received = exchange(message, "y")

    held, column_sum = call(
        split_kernel, "split", (shape(2, 4, 256, 128), shape(256, 128)), [VMEM]
    )(received)
    column_sum = lax.ppermute(column_sum, REP + ROW, [(d, s) for s, d in PAIRS])
    dense = call(dense_kernel, "dense", shape(1024, 2048), [SMEM, SMEM, VMEM])(
        counts, cols, tiles
    )
    held, dense = lax.optimization_barrier((held, dense))
    held = exchange(held, "c")
    message = call(
        lambda *refs: forward_kernel(scaling, *refs),
        "forward",
        shape(16, 80, 128),
        [VMEM] * 3,
        [pltpu.VMEM((1024, 128), F32)],
        flops=2 * 128 * 1024 * 2304,
        moved=3 << 20,
    )(dense, held, node_grad)
    message = jnp.concatenate([message, column_sum.reshape(16, 16, 128)], axis=1)
    parts = exchange(message, REP)

    piece, weight_part = call(
        reduce_kernel, "reduce", (shape(128, 128), shape(32, 16, 128)), [VMEM]
    )(parts)
    weight_parts = exchange(weight_part, ROW)
    message = call(gather_kernel, "gather", shape(16, 144, 128), [VMEM] * 2)(piece, weight_parts)
    received = exchange(message, REP)
    return call(
        output_kernel,
        "output",
        (shape(1024, 256), shape(128, 256, dtype=F32), shape(1024, 128)),
        [SMEM, VMEM, VMEM],
    )(order, received, weight)


def solution(mesh):
    fine = Mesh(mesh.devices.reshape(4, 4, 4, 4, 2), REP + ROW)
    placed = (
        P(ROW, None),
        P(REP, ROW, None, None, None),
        P(REP, ROW, None),
        P(REP, ROW, None),
        P(),
        P(ROW, None),
    )
    return jax.shard_map(
        body,
        mesh=fine,
        in_specs=placed,
        out_specs=(P(ROW, None), P(), P(ROW, None)),
        check_vma=False,
    )
```

```python
import math

import jax
import jax.numpy as jnp
import numpy as np
from jax import lax
from jax.experimental import pallas as pl
from jax.experimental.pallas import tpu as pltpu
from jax.sharding import Mesh
from jax.sharding import PartitionSpec as P

REP = ("zl", "x")
ROW = ("zh", "y", "c")
F32 = jnp.float32
BF16 = jnp.bfloat16
VMEM = pl.BlockSpec(memory_space=pltpu.VMEM)
SMEM = pl.BlockSpec(memory_space=pltpu.SMEM)
HBM = pl.BlockSpec(memory_space=pltpu.HBM)

NEAR = ((1, 2, 3, 0), (2, 3, 0, 1))


def chunk(q, zh, k):
    step = (k // 2 - q // 2) % 4
    near_half = int((zh - q // 8) % 4 < 2)
    half = near_half if step < 2 else 1 - near_half
    return half * 4 + (0 if step in (1, 2) else 2) + k % 2


def pair(q, zh, k):
    half, quarter = divmod(chunk(q, zh, k), 4)
    a = NEAR[q // 8][(zh - half * 2 - q // 8) % 4] * 4 + (q + quarter) % 4
    return a * 32 + q + half * 16, q * 32 + zh * 8 + k


PAIRS = [pair(q, zh, k) for q in range(16) for zh in range(4) for k in range(8)]
CHUNKS = np.array(
    [[[chunk(q, zh, k) for k in range(8)] for zh in range(4)] for q in range(16)], np.int32
)


def shape(*dims, dtype=BF16):
    return jax.ShapeDtypeStruct(dims, dtype)


def columns(dense, index):
    return dense[:, pl.ds(pl.multiple_of(index * 256, 256), 256)]


def fill(counts, cols, tiles, dense):
    def clear(b, carry):
        dense[pl.ds(pl.multiple_of(b * 128, 128), 128), :] = jnp.zeros((128, 2048), BF16)
        return carry

    lax.fori_loop(0, 8, clear, 0)
    yield
    start = jnp.int32(0)
    for b in range(8):
        count = counts[b]

        def place(i, carry, b=b, start=start):
            slot = start + i
            col = pl.multiple_of(cols[slot] * 128, 128)
            dense[b * 128 : (b + 1) * 128, pl.ds(col, 128)] = tiles[slot]
            return carry

        lax.fori_loop(0, count, place, 0)
        start = start + count
    yield


def tile_copies(tiles_hbm, tiles, sems):
    return [
        pltpu.make_async_copy(
            tiles_hbm.at[pl.ds(i * 12, 12)], tiles.at[pl.ds(i * 12, 12)], sems.at[i]
        )
        for i in range(8)
    ]


def backward_kernel(
    chunks, counts, cols, tiles_hbm, grad_hbm, weight_hbm, terms,
    tiles, node_grad, weight, dense, grad_t, sems,
):
    copies = [
        pltpu.make_async_copy(weight_hbm, weight, sems.at[8]),
        pltpu.make_async_copy(grad_hbm, node_grad, sems.at[9]),
    ]
    loads = tile_copies(tiles_hbm, tiles, sems)
    for copy in copies + loads:
        copy.start()
    filling = fill(counts, cols, tiles, dense)
    next(filling)
    copies[0].wait()
    copies[1].wait()
    grad_t[...] = lax.dot_general(
        weight[...], node_grad[...], (((1,), (1,)), ((), ())), preferred_element_type=F32
    ).astype(BF16)
    for copy in loads:
        copy.wait()
    next(filling)
    for k in range(8):
        term = jnp.dot(grad_t[...], columns(dense, chunks[k]), preferred_element_type=F32)
        terms[k % 2, k // 2] = term.T.astype(BF16)


def pack_kernel(terms, quarter, message):
    for y in range(4):
        message[y, 0:256, :] = quarter[...]
        message[y, 256:512, :] = (terms[0, y].astype(F32) + terms[1, y].astype(F32)).astype(BF16)


def split_kernel(received, held, column_sum):
    total = received[0, 256:512, :].astype(F32)
    for y in range(1, 4):
        total = total + received[y, 256:512, :].astype(F32)
    column_sum[...] = total.astype(BF16)
    for c in range(2):
        held[c] = received[:, 0:256, :]


def dense_kernel(counts, cols, tiles, dense):
    for _ in fill(counts, cols, tiles, dense):
        pass


def forward_kernel(scaling, chunks, dense, held, node_grad, message, total):
    for k in range(8):
        term = jnp.dot(
            columns(dense, chunks[k]), held[k % 2, k // 2], preferred_element_type=F32
        )
        if k == 0:
            total[...] = term
        else:
            total[...] += term
    partial = total[...].astype(BF16)
    message[:, 0:64, :] = partial.reshape(16, 64, 128)
    term = lax.dot_general(
        partial, node_grad[...], (((0,), (0,)), ((), ())), preferred_element_type=F32
    )
    term = term * scaling
    message[:, 64:80, :] = jnp.concatenate(
        [term[:, 0:128].reshape(16, 8, 128), term[:, 128:256].reshape(16, 8, 128)], axis=1
    ).astype(BF16)


def reduce_kernel(parts, piece, weight_part):
    total = parts[0, 0:64, :].astype(F32)
    for a in range(1, 16):
        total = total + parts[a, 0:64, :].astype(F32)
    piece[0:64, :] = total.astype(BF16)
    for part in range(4):
        total = parts[part, 80:96, :].astype(F32)
        for zl in range(1, 4):
            total = total + parts[zl * 4 + part, 80:96, :].astype(F32)
        piece[64 + part * 16 : 80 + part * 16, :] = total.astype(BF16)
    total = parts[0, 64:80, :].astype(F32)
    for a in range(1, 16):
        total = total + parts[a, 64:80, :].astype(F32)
    weight_part[...] = jnp.broadcast_to(total.astype(BF16)[None], (32, 16, 128))


def gather_kernel(piece, weight_parts, message):
    message[:, 0:128, :] = jnp.broadcast_to(piece[...][None], (16, 128, 128))
    total = weight_parts[0].astype(F32)
    for r in range(1, 32):
        total = total + weight_parts[r].astype(F32)
    message[:, 128:144, :] = jnp.broadcast_to(total.astype(BF16)[None], (16, 16, 128))


def output_kernel(order, received, weight, output, weight_grad, feature_grad):
    parts = received[:, 128:144, :].astype(F32)
    weight_grad[:, 0:128] = parts[:, 0:8, :].reshape(128, 128)
    weight_grad[:, 128:256] = parts[:, 8:16, :].reshape(128, 128)
    for zq in range(4):
        aggregate = received[zq * 4 : zq * 4 + 4, 0:64, :].reshape(256, 128)
        output[zq * 256 : (zq + 1) * 256, :] = jnp.dot(
            aggregate, weight[...], preferred_element_type=F32
        ).astype(BF16)
        row = pl.multiple_of(order[zq] * 256, 256)
        feature_grad[pl.ds(row, 256), :] = received[
            :, 64 + zq * 16 : 80 + zq * 16, :
        ].reshape(256, 128)


def call(kernel, name, outs, ins, scratch=(), flops=0, moved=1 << 20, limit=16):
    return pl.pallas_call(
        kernel,
        out_shape=outs,
        in_specs=ins,
        out_specs=jax.tree.map(lambda _: VMEM, outs),
        scratch_shapes=list(scratch),
        compiler_params=pltpu.CompilerParams(vmem_limit_bytes=limit << 20),
        cost_estimate=pl.CostEstimate(flops=flops, bytes_accessed=moved, transcendentals=0),
        name=name,
    )


def exchange(block, axes):
    return lax.all_to_all(block, axes, 0, 0)


def body(features, tile_values, tile_counts, tile_columns, weight, node_grad):
    rep_index = lax.axis_index(REP)
    row_index = lax.axis_index(ROW)
    scaling = 1.0 / math.sqrt(features.shape[0] * 32)
    counts, cols, tiles = tile_counts[0, 0], tile_columns[0, 0], tile_values[0, 0]
    order = (jnp.arange(4, dtype=jnp.int32) - row_index) & 3
    chunks = jnp.asarray(CHUNKS)[rep_index, lax.axis_index("zh")]

    terms = call(
        backward_kernel,
        "backward",
        shape(2, 4, 256, 128),
        [SMEM, SMEM, SMEM, HBM, HBM, HBM],
        [
            pltpu.VMEM((96, 128, 128), BF16),
            pltpu.VMEM((1024, 256), BF16),
            pltpu.VMEM((128, 256), BF16),
            pltpu.VMEM((1024, 2048), BF16),
            pltpu.VMEM((128, 1024), BF16),
            pltpu.SemaphoreType.DMA((10,)),
        ],
        flops=2 * 128 * 1024 * 2304,
        moved=8 << 20,
        limit=58,
    )(chunks, counts, cols, tiles, node_grad, weight)
    start = ((rep_index - row_index) & 3) * 256
    quarter = lax.dynamic_slice_in_dim(features, start, 256, axis=0)
    quarter = lax.ppermute(quarter, REP + ROW, PAIRS)
    terms = exchange(terms, "c")
    message = call(pack_kernel, "pack", shape(4, 512, 128), [VMEM] * 2)(terms, quarter)
    received = exchange(message, "y")

    held, column_sum = call(
        split_kernel, "split", (shape(2, 4, 256, 128), shape(256, 128)), [VMEM]
    )(received)
    column_sum = lax.ppermute(column_sum, REP + ROW, [(d, s) for s, d in PAIRS])
    dense = call(dense_kernel, "dense", shape(1024, 2048), [SMEM, SMEM, VMEM])(
        counts, cols, tiles
    )
    held, dense = lax.optimization_barrier((held, dense))
    held = exchange(held, "c")
    message = call(
        lambda *refs: forward_kernel(scaling, *refs),
        "forward",
        shape(16, 80, 128),
        [SMEM] + [VMEM] * 3,
        [pltpu.VMEM((1024, 128), F32)],
        flops=2 * 128 * 1024 * 2304,
        moved=3 << 20,
    )(chunks, dense, held, node_grad)
    message = jnp.concatenate([message, column_sum.reshape(16, 16, 128)], axis=1)
    parts = exchange(message, REP)

    piece, weight_part = call(
        reduce_kernel, "reduce", (shape(128, 128), shape(32, 16, 128)), [VMEM]
    )(parts)
    weight_parts = exchange(weight_part, ROW)
    message = call(gather_kernel, "gather", shape(16, 144, 128), [VMEM] * 2)(piece, weight_parts)
    received = exchange(message, REP)
    return call(
        output_kernel,
        "output",
        (shape(1024, 256), shape(128, 256, dtype=F32), shape(1024, 128)),
        [SMEM, VMEM, VMEM],
    )(order, received, weight)


def solution(mesh):
    fine = Mesh(mesh.devices.reshape(4, 4, 4, 4, 2), REP + ROW)
    placed = (
        P(ROW, None),
        P(REP, ROW, None, None, None),
        P(REP, ROW, None),
        P(REP, ROW, None),
        P(),
        P(ROW, None),
    )
    return jax.shard_map(
        body,
        mesh=fine,
        in_specs=placed,
        out_specs=(P(ROW, None), P(), P(ROW, None)),
        check_vma=False,
    )
```

```python
import math

import jax
import jax.numpy as jnp
from jax import lax
from jax.experimental import pallas as pl
from jax.experimental.pallas import tpu as pltpu
from jax.sharding import Mesh
from jax.sharding import PartitionSpec as P

REP = ("zl", "x")
ROW = ("zh", "y", "c")
YC = ("y", "c")
F32 = jnp.float32
BF16 = jnp.bfloat16
VMEM = pl.BlockSpec(memory_space=pltpu.VMEM)
SMEM = pl.BlockSpec(memory_space=pltpu.SMEM)
HBM = pl.BlockSpec(memory_space=pltpu.HBM)

NEAR = ((1, 2, 3, 0), (2, 3, 0, 1))


def farther(q, half):
    return 1 - (((q >> 1) + 1) >> 1 & 1) ^ half


def pair(q, zh, k):
    half, turn = k // 4, k % 2
    if k // 2 % 2 != farther(q, half):
        turn += 2
    a = NEAR[q // 8][(zh - half * 2 - q // 8) % 4] * 4 + (q + turn) % 4
    return a * 32 + q + half * 16, q * 32 + zh * 8 + k


def quarter_of(a, s):
    turn = (a - s) % 4
    far = farther(s % 16, s // 16)
    return jnp.where(turn < 2, far, 1 - far) * 2 + turn % 2


PAIRS = [pair(q, zh, k) for q in range(16) for zh in range(4) for k in range(8)]


def shape(*dims, dtype=BF16):
    return jax.ShapeDtypeStruct(dims, dtype)


def fill(counts, cols, tiles, dense):
    def clear(b, carry):
        dense[pl.ds(pl.multiple_of(b * 128, 128), 128), :] = jnp.zeros((128, 2048), BF16)
        return carry

    lax.fori_loop(0, 8, clear, 0)
    yield
    start = jnp.int32(0)
    for b in range(8):
        count = counts[b]

        def place(i, carry, b=b, start=start):
            slot = start + i
            col = pl.multiple_of(cols[slot] * 128, 128)
            dense[b * 128 : (b + 1) * 128, pl.ds(col, 128)] = tiles[slot]
            return carry

        lax.fori_loop(0, count, place, 0)
        start = start + count
    yield


def tile_copies(tiles_hbm, tiles, sems):
    return [
        pltpu.make_async_copy(
            tiles_hbm.at[pl.ds(i * 12, 12)], tiles.at[pl.ds(i * 12, 12)], sems.at[i]
        )
        for i in range(8)
    ]


def backward_kernel(
    counts, cols, tiles_hbm, grad_hbm, weight_hbm, terms,
    tiles, node_grad, weight, dense, grad_t, sems,
):
    copies = [
        pltpu.make_async_copy(weight_hbm, weight, sems.at[8]),
        pltpu.make_async_copy(grad_hbm, node_grad, sems.at[9]),
    ]
    loads = tile_copies(tiles_hbm, tiles, sems)
    for copy in copies + loads:
        copy.start()
    filling = fill(counts, cols, tiles, dense)
    next(filling)
    copies[0].wait()
    copies[1].wait()
    grad_t[...] = lax.dot_general(
        weight[...], node_grad[...], (((1,), (1,)), ((), ())), preferred_element_type=F32
    ).astype(BF16)
    for copy in loads:
        copy.wait()
    next(filling)
    for k in range(8):
        term = jnp.dot(
            grad_t[...], dense[:, k * 256 : (k + 1) * 256], preferred_element_type=F32
        )
        terms[k % 2, k // 2] = term.T.astype(BF16)


def pack_kernel(terms, quarter, message):
    for y in range(4):
        message[y, 0:256, :] = quarter[...]
        message[y, 256:512, :] = (terms[0, y].astype(F32) + terms[1, y].astype(F32)).astype(BF16)


def split_kernel(received, held, column_sum):
    total = received[0, 256:512, :].astype(F32)
    for y in range(1, 4):
        total = total + received[y, 256:512, :].astype(F32)
    column_sum[...] = total.astype(BF16)
    for c in range(2):
        held[c] = received[:, 0:256, :]


def dense_kernel(counts, cols, tiles, dense):
    for _ in fill(counts, cols, tiles, dense):
        pass


def forward_kernel(scaling, dense, held, node_grad, message, total):
    for k in range(8):
        term = jnp.dot(
            dense[:, k * 256 : (k + 1) * 256], held[k % 2, k // 2], preferred_element_type=F32
        )
        if k == 0:
            total[...] = term
        else:
            total[...] += term
    partial = total[...].astype(BF16)
    message[:, 0:64, :] = partial.reshape(16, 64, 128)
    term = lax.dot_general(
        partial, node_grad[...], (((0,), (0,)), ((), ())), preferred_element_type=F32
    )
    term = term * scaling
    message[:, 64:80, :] = jnp.concatenate(
        [term[:, 0:128].reshape(16, 8, 128), term[:, 128:256].reshape(16, 8, 128)], axis=1
    ).astype(BF16)


def reduce_kernel(parts, piece, weight_part):
    total = parts[0, 0:64, :].astype(F32)
    for a in range(1, 16):
        total = total + parts[a, 0:64, :].astype(F32)
    piece[0:64, :] = total.astype(BF16)
    for part in range(4):
        total = parts[part, 80:96, :].astype(F32)
        for zl in range(1, 4):
            total = total + parts[zl * 4 + part, 80:96, :].astype(F32)
        piece[64 + part * 16 : 80 + part * 16, :] = total.astype(BF16)
    total = parts[0, 64:80, :].astype(F32)
    for a in range(1, 16):
        total = total + parts[a, 64:80, :].astype(F32)
    weight_part[...] = jnp.broadcast_to(total.astype(BF16)[None], (8, 16, 128))


def weight_kernel(parts, total):
    partial = parts[0].astype(F32)
    for k in range(1, 8):
        partial = partial + parts[k].astype(F32)
    total[...] = jnp.broadcast_to(partial[None], (4, 16, 128))


def gather_kernel(piece, weight_parts, message):
    message[:, 0:128, :] = jnp.broadcast_to(piece[...][None], (16, 128, 128))
    total = (weight_parts[0] + weight_parts[1]) + (weight_parts[2] + weight_parts[3])
    message[:, 128:144, :] = jnp.broadcast_to(total.astype(BF16)[None], (16, 16, 128))


def output_kernel(order, received, weight, output, weight_grad, feature_grad):
    parts = received[:, 128:144, :].astype(F32)
    weight_grad[:, 0:128] = parts[:, 0:8, :].reshape(128, 128)
    weight_grad[:, 128:256] = parts[:, 8:16, :].reshape(128, 128)
    for zq in range(4):
        aggregate = received[zq * 4 : zq * 4 + 4, 0:64, :].reshape(256, 128)
        output[zq * 256 : (zq + 1) * 256, :] = jnp.dot(
            aggregate, weight[...], preferred_element_type=F32
        ).astype(BF16)
        row = pl.multiple_of(order[zq] * 256, 256)
        feature_grad[pl.ds(row, 256), :] = received[
            :, 64 + zq * 16 : 80 + zq * 16, :
        ].reshape(256, 128)


def call(kernel, name, outs, ins, scratch=(), flops=0, moved=1 << 20, limit=16):
    return pl.pallas_call(
        kernel,
        out_shape=outs,
        in_specs=ins,
        out_specs=jax.tree.map(lambda _: VMEM, outs),
        scratch_shapes=list(scratch),
        compiler_params=pltpu.CompilerParams(vmem_limit_bytes=limit << 20),
        cost_estimate=pl.CostEstimate(flops=flops, bytes_accessed=moved, transcendentals=0),
        name=name,
    )


def exchange(block, axes):
    return lax.all_to_all(block, axes, 0, 0)


def body(features, tile_values, tile_counts, tile_columns, weight, node_grad):
    rep_index = lax.axis_index(REP)
    row_index = lax.axis_index(ROW)
    scaling = 1.0 / math.sqrt(features.shape[0] * 32)
    counts, cols, tiles = tile_counts[0, 0], tile_columns[0, 0], tile_values[0, 0]
    order = quarter_of(jnp.arange(4, dtype=jnp.int32), row_index).astype(jnp.int32)

    terms = call(
        backward_kernel,
        "backward",
        shape(2, 4, 256, 128),
        [SMEM, SMEM, HBM, HBM, HBM],
        [
            pltpu.VMEM((96, 128, 128), BF16),
            pltpu.VMEM((1024, 256), BF16),
            pltpu.VMEM((128, 256), BF16),
            pltpu.VMEM((1024, 2048), BF16),
            pltpu.VMEM((128, 1024), BF16),
            pltpu.SemaphoreType.DMA((10,)),
        ],
        flops=2 * 128 * 1024 * 2304,
        moved=8 << 20,
        limit=58,
    )(counts, cols, tiles, node_grad, weight)
    start = quarter_of(rep_index, row_index) * 256
    quarter = lax.dynamic_slice_in_dim(features, start, 256, axis=0)
    quarter = lax.ppermute(quarter, REP + ROW, PAIRS)
    terms = exchange(terms, "c")
    message = call(pack_kernel, "pack", shape(4, 512, 128), [VMEM] * 2)(terms, quarter)
    received = exchange(message, "y")

    held, column_sum = call(
        split_kernel, "split", (shape(2, 4, 256, 128), shape(256, 128)), [VMEM]
    )(received)
    column_sum = lax.ppermute(column_sum, REP + ROW, [(d, s) for s, d in PAIRS])
    dense = call(dense_kernel, "dense", shape(1024, 2048), [SMEM, SMEM, VMEM])(
        counts, cols, tiles
    )
    held, dense = lax.optimization_barrier((held, dense))
    held = exchange(held, "c")
    message = call(
        lambda *refs: forward_kernel(scaling, *refs),
        "forward",
        shape(16, 80, 128),
        [VMEM] * 3,
        [pltpu.VMEM((1024, 128), F32)],
        flops=2 * 128 * 1024 * 2304,
        moved=3 << 20,
    )(dense, held, node_grad)
    message = jnp.concatenate([message, column_sum.reshape(16, 16, 128)], axis=1)
    parts = exchange(message, REP)

    piece, weight_part = call(
        reduce_kernel, "reduce", (shape(128, 128), shape(8, 16, 128)), [VMEM]
    )(parts)
    weight_part = call(weight_kernel, "weight", shape(4, 16, 128, dtype=F32), [VMEM])(
        exchange(weight_part, YC)
    )
    weight_parts = exchange(weight_part, "zh")
    message = call(gather_kernel, "gather", shape(16, 144, 128), [VMEM] * 2)(piece, weight_parts)
    received = exchange(message, REP)
    return call(
        output_kernel,
        "output",
        (shape(1024, 256), shape(128, 256, dtype=F32), shape(1024, 128)),
        [SMEM, VMEM, VMEM],
    )(order, received, weight)


def solution(mesh):
    fine = Mesh(mesh.devices.reshape(4, 4, 4, 4, 2), REP + ROW)
    placed = (
        P(ROW, None),
        P(REP, ROW, None, None, None),
        P(REP, ROW, None),
        P(REP, ROW, None),
        P(),
        P(ROW, None),
    )
    return jax.shard_map(
        body,
        mesh=fine,
        in_specs=placed,
        out_specs=(P(ROW, None), P(), P(ROW, None)),
        check_vma=False,
    )
```

```python
import math

import jax
import jax.numpy as jnp
from jax import lax
from jax.experimental import pallas as pl
from jax.experimental.pallas import tpu as pltpu
from jax.sharding import Mesh
from jax.sharding import PartitionSpec as P

REP = ("zl", "x")
ROW = ("zh", "y", "c")
F32 = jnp.float32
BF16 = jnp.bfloat16
VMEM = pl.BlockSpec(memory_space=pltpu.VMEM)
SMEM = pl.BlockSpec(memory_space=pltpu.SMEM)
HBM = pl.BlockSpec(memory_space=pltpu.HBM)

NEAR = ((1, 2, 3, 0), (2, 3, 0, 1))


def farther(q, half):
    return 1 - (((q >> 1) + 1) >> 1 & 1) ^ half


def pair(q, zh, k):
    half, turn = k // 4, k % 2
    if k // 2 % 2 != farther(q, half):
        turn += 2
    a = NEAR[q // 8][(zh - half * 2 - q // 8) % 4] * 4 + (q + turn) % 4
    return a * 32 + q + half * 16, q * 32 + zh * 8 + k


def quarter_of(a, s):
    turn = (a - s) % 4
    far = farther(s % 16, s // 16)
    return jnp.where(turn < 2, far, 1 - far) * 2 + turn % 2


def back_pair(q, zh, k):
    return q * 32 + zh * 8 + k, (k % 4 * 4 + zh) * 32 + q + k // 4 * 16


BACK = [back_pair(q, zh, k) for q in range(16) for zh in range(4) for k in range(8)]
PAIRS = [pair(q, zh, k) for q in range(16) for zh in range(4) for k in range(8)]


def shape(*dims, dtype=BF16):
    return jax.ShapeDtypeStruct(dims, dtype)


def fill(counts, cols, tiles, dense):
    def clear(b, carry):
        dense[pl.ds(pl.multiple_of(b * 128, 128), 128), :] = jnp.zeros((128, 2048), BF16)
        return carry

    lax.fori_loop(0, 8, clear, 0)
    yield
    start = jnp.int32(0)
    for b in range(8):
        count = counts[b]

        def place(i, carry, b=b, start=start):
            slot = start + i
            col = pl.multiple_of(cols[slot] * 128, 128)
            dense[b * 128 : (b + 1) * 128, pl.ds(col, 128)] = tiles[slot]
            return carry

        lax.fori_loop(0, count, place, 0)
        start = start + count
    yield


def tile_copies(tiles_hbm, tiles, sems):
    return [
        pltpu.make_async_copy(
            tiles_hbm.at[pl.ds(i * 12, 12)], tiles.at[pl.ds(i * 12, 12)], sems.at[i]
        )
        for i in range(8)
    ]


def backward_kernel(
    counts, cols, tiles_hbm, grad_hbm, weight_hbm, terms,
    tiles, node_grad, weight, dense, grad_t, sems,
):
    copies = [
        pltpu.make_async_copy(weight_hbm, weight, sems.at[8]),
        pltpu.make_async_copy(grad_hbm, node_grad, sems.at[9]),
    ]
    loads = tile_copies(tiles_hbm, tiles, sems)
    for copy in copies + loads:
        copy.start()
    filling = fill(counts, cols, tiles, dense)
    next(filling)
    copies[0].wait()
    copies[1].wait()
    grad_t[...] = lax.dot_general(
        weight[...], node_grad[...], (((1,), (1,)), ((), ())), preferred_element_type=F32
    ).astype(BF16)
    for copy in loads:
        copy.wait()
    next(filling)
    for k in range(8):
        term = jnp.dot(
            grad_t[...], dense[:, k * 256 : (k + 1) * 256], preferred_element_type=F32
        )
        terms[k % 2, k // 2] = term.T.astype(BF16)


def pack_kernel(terms, quarter, message):
    for y in range(4):
        message[y, 0:256, :] = quarter[...]
        message[y, 256:512, :] = (terms[0, y].astype(F32) + terms[1, y].astype(F32)).astype(BF16)


def split_kernel(received, held, column_sum):
    total = received[0, 256:512, :].astype(F32)
    for y in range(1, 4):
        total = total + received[y, 256:512, :].astype(F32)
    column_sum[...] = total.astype(BF16)
    for c in range(2):
        held[c] = received[:, 0:256, :]


def dense_kernel(counts, cols, tiles, dense):
    for _ in fill(counts, cols, tiles, dense):
        pass


def forward_kernel(scaling, dense, held, node_grad, message, total):
    for k in range(8):
        term = jnp.dot(
            dense[:, k * 256 : (k + 1) * 256], held[k % 2, k // 2], preferred_element_type=F32
        )
        if k == 0:
            total[...] = term
        else:
            total[...] += term
    partial = total[...].astype(BF16)
    message[:, 0:64, :] = partial.reshape(16, 64, 128)
    term = lax.dot_general(
        partial, node_grad[...], (((0,), (0,)), ((), ())), preferred_element_type=F32
    )
    term = term * scaling
    message[:, 64:80, :] = jnp.concatenate(
        [term[:, 0:128].reshape(16, 8, 128), term[:, 128:256].reshape(16, 8, 128)], axis=1
    ).astype(BF16)


def reduce_kernel(parts, piece, weight_part):
    total = parts[0].astype(F32)
    for a in range(1, 16):
        total = total + parts[a].astype(F32)
    piece[...] = total[0:64].astype(BF16)
    weight_part[...] = jnp.broadcast_to(total[64:80].astype(BF16)[None], (32, 16, 128))


def slice_kernel(place, column, *slices):
    for k in range(4):
        row = pl.multiple_of(((place[0] + k) & 3) * 64, 64)
        slices[k][...] = column[pl.ds(row, 64), :]


def gather_kernel(piece, own, first, second, third, weight_parts, message):
    message[:, 0:64, :] = jnp.broadcast_to(piece[...][None], (16, 64, 128))
    column = (own[...].astype(F32) + first[...].astype(F32)) + (
        second[...].astype(F32) + third[...].astype(F32)
    )
    message[:, 64:128, :] = jnp.broadcast_to(column.astype(BF16)[None], (16, 64, 128))
    total = weight_parts[0].astype(F32)
    for r in range(1, 32):
        total = total + weight_parts[r].astype(F32)
    message[:, 128:144, :] = jnp.broadcast_to(total.astype(BF16)[None], (16, 16, 128))


def output_kernel(received, weight, output, weight_grad, feature_grad):
    parts = received[:, 128:144, :].astype(F32)
    weight_grad[:, 0:128] = parts[:, 0:8, :].reshape(128, 128)
    weight_grad[:, 128:256] = parts[:, 8:16, :].reshape(128, 128)
    feature_grad[...] = received[:, 64:128, :].reshape(1024, 128)
    for quarter in range(4):
        aggregate = received[quarter * 4 : quarter * 4 + 4, 0:64, :].reshape(256, 128)
        output[quarter * 256 : (quarter + 1) * 256, :] = jnp.dot(
            aggregate, weight[...], preferred_element_type=F32
        ).astype(BF16)


def call(kernel, name, outs, ins, scratch=(), flops=0, moved=1 << 20, limit=16):
    return pl.pallas_call(
        kernel,
        out_shape=outs,
        in_specs=ins,
        out_specs=jax.tree.map(lambda _: VMEM, outs),
        scratch_shapes=list(scratch),
        compiler_params=pltpu.CompilerParams(vmem_limit_bytes=limit << 20),
        cost_estimate=pl.CostEstimate(flops=flops, bytes_accessed=moved, transcendentals=0),
        name=name,
    )


def exchange(block, axes):
    return lax.all_to_all(block, axes, 0, 0)


def body(features, tile_values, tile_counts, tile_columns, weight, node_grad):
    rep_index = lax.axis_index(REP)
    row_index = lax.axis_index(ROW)
    scaling = 1.0 / math.sqrt(features.shape[0] * 32)
    counts, cols, tiles = tile_counts[0, 0], tile_columns[0, 0], tile_values[0, 0]
    place = lax.axis_index("x").astype(jnp.int32).reshape(1)

    terms = call(
        backward_kernel,
        "backward",
        shape(2, 4, 256, 128),
        [SMEM, SMEM, HBM, HBM, HBM],
        [
            pltpu.VMEM((96, 128, 128), BF16),
            pltpu.VMEM((1024, 256), BF16),
            pltpu.VMEM((128, 256), BF16),
            pltpu.VMEM((1024, 2048), BF16),
            pltpu.VMEM((128, 1024), BF16),
            pltpu.SemaphoreType.DMA((10,)),
        ],
        flops=2 * 128 * 1024 * 2304,
        moved=8 << 20,
        limit=58,
    )(counts, cols, tiles, node_grad, weight)
    start = quarter_of(rep_index, row_index) * 256
    quarter = lax.dynamic_slice_in_dim(features, start, 256, axis=0)
    quarter = lax.ppermute(quarter, REP + ROW, PAIRS)
    terms = exchange(terms, "c")
    message = call(pack_kernel, "pack", shape(4, 512, 128), [VMEM] * 2)(terms, quarter)
    received = exchange(message, "y")

    held, column_sum = call(
        split_kernel, "split", (shape(2, 4, 256, 128), shape(256, 128)), [VMEM]
    )(received)
    column_sum = lax.ppermute(column_sum, REP + ROW, BACK)
    counts, held = lax.optimization_barrier((counts, held))
    dense = call(dense_kernel, "dense", shape(1024, 2048), [SMEM, SMEM, VMEM])(
        counts, cols, tiles
    )
    held, dense = lax.optimization_barrier((held, dense))
    held = exchange(held, "c")
    message = call(
        lambda *refs: forward_kernel(scaling, *refs),
        "forward",
        shape(16, 80, 128),
        [VMEM] * 3,
        [pltpu.VMEM((1024, 128), F32)],
        flops=2 * 128 * 1024 * 2304,
        moved=3 << 20,
    )(dense, held, node_grad)
    parts = exchange(message, REP)
    parts, column_sum = lax.optimization_barrier((parts, column_sum))

    piece, weight_part = call(
        reduce_kernel, "reduce", (shape(64, 128), shape(32, 16, 128)), [VMEM]
    )(parts)
    weight_parts = exchange(weight_part, ROW)
    own, *others = call(slice_kernel, "slice", (shape(64, 128),) * 4, [SMEM, VMEM])(
        place, column_sum
    )
    others = [
        lax.ppermute(block, "x", [(i, (i + k + 1) % 4) for i in range(4)])
        for k, block in enumerate(others)
    ]
    message = call(gather_kernel, "gather", shape(16, 144, 128), [VMEM] * 6)(
        piece, own, *others, weight_parts
    )
    received = exchange(message, REP)
    return call(
        output_kernel,
        "output",
        (shape(1024, 256), shape(128, 256, dtype=F32), shape(1024, 128)),
        [VMEM] * 2,
    )(received, weight)


def solution(mesh):
    fine = Mesh(mesh.devices.reshape(4, 4, 4, 4, 2), REP + ROW)
    placed = (
        P(ROW, None),
        P(REP, ROW, None, None, None),
        P(REP, ROW, None),
        P(REP, ROW, None),
        P(),
        P(ROW, None),
    )
    return jax.shard_map(
        body,
        mesh=fine,
        in_specs=placed,
        out_specs=(P(ROW, None), P(), P(ROW, None)),
        check_vma=False,
    )
```

```python
import math

import jax
import jax.numpy as jnp
from jax import lax
from jax.experimental import pallas as pl
from jax.experimental.pallas import tpu as pltpu
from jax.sharding import Mesh
from jax.sharding import PartitionSpec as P

REP = ("zl", "x")
ROW = ("zh", "y", "c")
F32 = jnp.float32
BF16 = jnp.bfloat16
VMEM = pl.BlockSpec(memory_space=pltpu.VMEM)
SMEM = pl.BlockSpec(memory_space=pltpu.SMEM)
HBM = pl.BlockSpec(memory_space=pltpu.HBM)

NEAR = ((1, 2, 3, 0), (2, 3, 0, 1))


def farther(q, half):
    return 1 - (((q >> 1) + 1) >> 1 & 1) ^ half


def pair(q, zh, k):
    half, turn = k // 4, k % 2
    if k // 2 % 2 != farther(q, half):
        turn += 2
    a = NEAR[q // 8][(zh - half * 2 - q // 8) % 4] * 4 + (q + turn) % 4
    return a * 32 + q + half * 16, q * 32 + zh * 8 + k


def quarter_of(a, s):
    turn = (a - s) % 4
    far = farther(s % 16, s // 16)
    return jnp.where(turn < 2, far, 1 - far) * 2 + turn % 2


def back_pair(q, zh, k):
    half, u = k // 4, k % 2
    if k // 2 % 2 != farther(q, half):
        u += 2
    zl = u if q // 8 else 3 - u
    x = (q + (2, 1, 0, 3)[(zh - half * 2 - q // 8) % 4]) % 4
    return q * 32 + zh * 8 + k, (zl * 4 + x) * 32 + q + half * 16


def back_quarter(zl, s):
    u = jnp.where(s % 16 // 8 == 0, 3 - zl, zl)
    far = farther(s % 16, s // 16)
    return jnp.where(u < 2, far, 1 - far) * 2 + u % 2


BACK = [back_pair(q, zh, k) for q in range(16) for zh in range(4) for k in range(8)]
PAIRS = [pair(q, zh, k) for q in range(16) for zh in range(4) for k in range(8)]


def shape(*dims, dtype=BF16):
    return jax.ShapeDtypeStruct(dims, dtype)


def fill(counts, cols, tiles, dense):
    def clear(b, carry):
        dense[pl.ds(pl.multiple_of(b * 128, 128), 128), :] = jnp.zeros((128, 2048), BF16)
        return carry

    lax.fori_loop(0, 8, clear, 0)
    yield
    start = jnp.int32(0)
    for b in range(8):
        count = counts[b]

        def place(i, carry, b=b, start=start):
            slot = start + i
            col = pl.multiple_of(cols[slot] * 128, 128)
            dense[b * 128 : (b + 1) * 128, pl.ds(col, 128)] = tiles[slot]
            return carry

        lax.fori_loop(0, count, place, 0)
        start = start + count
    yield


def tile_copies(tiles_hbm, tiles, sems):
    return [
        pltpu.make_async_copy(
            tiles_hbm.at[pl.ds(i * 12, 12)], tiles.at[pl.ds(i * 12, 12)], sems.at[i]
        )
        for i in range(8)
    ]


def backward_kernel(
    counts, cols, tiles_hbm, grad_hbm, weight_hbm, terms,
    tiles, node_grad, weight, dense, grad_t, sems,
):
    copies = [
        pltpu.make_async_copy(weight_hbm, weight, sems.at[8]),
        pltpu.make_async_copy(grad_hbm, node_grad, sems.at[9]),
    ]
    loads = tile_copies(tiles_hbm, tiles, sems)
    for copy in copies + loads:
        copy.start()
    filling = fill(counts, cols, tiles, dense)
    next(filling)
    copies[0].wait()
    copies[1].wait()
    grad_t[...] = lax.dot_general(
        weight[...], node_grad[...], (((1,), (1,)), ((), ())), preferred_element_type=F32
    ).astype(BF16)
    for copy in loads:
        copy.wait()
    next(filling)
    for k in range(8):
        term = jnp.dot(
            grad_t[...], dense[:, k * 256 : (k + 1) * 256], preferred_element_type=F32
        )
        terms[k % 2, k // 2] = term.T.astype(BF16)


def pack_kernel(terms, quarter, message):
    for y in range(4):
        message[y, 0:256, :] = quarter[...]
        message[y, 256:512, :] = (terms[0, y].astype(F32) + terms[1, y].astype(F32)).astype(BF16)


def split_kernel(received, held, column_sum):
    total = received[0, 256:512, :].astype(F32)
    for y in range(1, 4):
        total = total + received[y, 256:512, :].astype(F32)
    column_sum[...] = total.astype(BF16)
    for c in range(2):
        held[c] = received[:, 0:256, :]


def dense_kernel(counts, cols, tiles, dense):
    for _ in fill(counts, cols, tiles, dense):
        pass


def forward_kernel(scaling, dense, held, node_grad, message, total):
    for k in range(8):
        term = jnp.dot(
            dense[:, k * 256 : (k + 1) * 256], held[k % 2, k // 2], preferred_element_type=F32
        )
        if k == 0:
            total[...] = term
        else:
            total[...] += term
    partial = total[...].astype(BF16)
    message[:, 0:64, :] = partial.reshape(16, 64, 128)
    term = lax.dot_general(
        partial, node_grad[...], (((0,), (0,)), ((), ())), preferred_element_type=F32
    )
    term = term * scaling
    message[:, 64:80, :] = jnp.concatenate(
        [term[:, 0:128].reshape(16, 8, 128), term[:, 128:256].reshape(16, 8, 128)], axis=1
    ).astype(BF16)


def reduce_kernel(parts, piece, weight_part):
    total = parts[0].astype(F32)
    for a in range(1, 16):
        total = total + parts[a].astype(F32)
    piece[...] = total[0:64].astype(BF16)
    weight_part[...] = jnp.broadcast_to(total[64:80].astype(BF16)[None], (32, 16, 128))


def slice_kernel(place, column, *slices):
    for k in range(4):
        row = pl.multiple_of(((place[0] + k) & 3) * 64, 64)
        slices[k][...] = column[pl.ds(row, 64), :]


def gather_kernel(piece, own, first, second, third, weight_parts, message):
    message[:, 0:64, :] = jnp.broadcast_to(piece[...][None], (16, 64, 128))
    column = (own[...].astype(F32) + first[...].astype(F32)) + (
        second[...].astype(F32) + third[...].astype(F32)
    )
    message[:, 64:128, :] = jnp.broadcast_to(column.astype(BF16)[None], (16, 64, 128))
    total = weight_parts[0].astype(F32)
    for r in range(1, 32):
        total = total + weight_parts[r].astype(F32)
    message[:, 128:144, :] = jnp.broadcast_to(total.astype(BF16)[None], (16, 16, 128))


def output_kernel(order, received, weight, output, weight_grad, feature_grad):
    parts = received[:, 128:144, :].astype(F32)
    weight_grad[:, 0:128] = parts[:, 0:8, :].reshape(128, 128)
    weight_grad[:, 128:256] = parts[:, 8:16, :].reshape(128, 128)
    for quarter in range(4):
        row = pl.multiple_of(order[quarter] * 256, 256)
        feature_grad[pl.ds(row, 256), :] = received[
            quarter * 4 : quarter * 4 + 4, 64:128, :
        ].reshape(256, 128)
        aggregate = received[quarter * 4 : quarter * 4 + 4, 0:64, :].reshape(256, 128)
        output[quarter * 256 : (quarter + 1) * 256, :] = jnp.dot(
            aggregate, weight[...], preferred_element_type=F32
        ).astype(BF16)


def call(kernel, name, outs, ins, scratch=(), flops=0, moved=1 << 20, limit=16):
    return pl.pallas_call(
        kernel,
        out_shape=outs,
        in_specs=ins,
        out_specs=jax.tree.map(lambda _: VMEM, outs),
        scratch_shapes=list(scratch),
        compiler_params=pltpu.CompilerParams(vmem_limit_bytes=limit << 20),
        cost_estimate=pl.CostEstimate(flops=flops, bytes_accessed=moved, transcendentals=0),
        name=name,
    )


def exchange(block, axes):
    return lax.all_to_all(block, axes, 0, 0)


def body(features, tile_values, tile_counts, tile_columns, weight, node_grad):
    rep_index = lax.axis_index(REP)
    row_index = lax.axis_index(ROW)
    scaling = 1.0 / math.sqrt(features.shape[0] * 32)
    counts, cols, tiles = tile_counts[0, 0], tile_columns[0, 0], tile_values[0, 0]
    order = back_quarter(jnp.arange(4, dtype=jnp.int32), row_index).astype(jnp.int32)
    place = lax.axis_index("x").astype(jnp.int32).reshape(1)

    terms = call(
        backward_kernel,
        "backward",
        shape(2, 4, 256, 128),
        [SMEM, SMEM, HBM, HBM, HBM],
        [
            pltpu.VMEM((96, 128, 128), BF16),
            pltpu.VMEM((1024, 256), BF16),
            pltpu.VMEM((128, 256), BF16),
            pltpu.VMEM((1024, 2048), BF16),
            pltpu.VMEM((128, 1024), BF16),
            pltpu.SemaphoreType.DMA((10,)),
        ],
        flops=2 * 128 * 1024 * 2304,
        moved=8 << 20,
        limit=58,
    )(counts, cols, tiles, node_grad, weight)
    start = quarter_of(rep_index, row_index) * 256
    quarter = lax.dynamic_slice_in_dim(features, start, 256, axis=0)
    quarter = lax.ppermute(quarter, REP + ROW, PAIRS)
    terms = exchange(terms, "c")
    message = call(pack_kernel, "pack", shape(4, 512, 128), [VMEM] * 2)(terms, quarter)
    received = exchange(message, "y")

    held, column_sum = call(
        split_kernel, "split", (shape(2, 4, 256, 128), shape(256, 128)), [VMEM]
    )(received)
    column_sum = lax.ppermute(column_sum, REP + ROW, BACK)
    counts, held = lax.optimization_barrier((counts, held))
    dense = call(dense_kernel, "dense", shape(1024, 2048), [SMEM, SMEM, VMEM])(
        counts, cols, tiles
    )
    held, dense = lax.optimization_barrier((held, dense))
    held = exchange(held, "c")
    message = call(
        lambda *refs: forward_kernel(scaling, *refs),
        "forward",
        shape(16, 80, 128),
        [VMEM] * 3,
        [pltpu.VMEM((1024, 128), F32)],
        flops=2 * 128 * 1024 * 2304,
        moved=3 << 20,
    )(dense, held, node_grad)
    parts = exchange(message, REP)
    parts, column_sum = lax.optimization_barrier((parts, column_sum))

    piece, weight_part = call(
        reduce_kernel, "reduce", (shape(64, 128), shape(32, 16, 128)), [VMEM]
    )(parts)
    weight_parts = exchange(weight_part, ROW)
    own, *others = call(slice_kernel, "slice", (shape(64, 128),) * 4, [SMEM, VMEM])(
        place, column_sum
    )
    others = [
        lax.ppermute(block, "x", [(i, (i + k + 1) % 4) for i in range(4)])
        for k, block in enumerate(others)
    ]
    message = call(gather_kernel, "gather", shape(16, 144, 128), [VMEM] * 6)(
        piece, own, *others, weight_parts
    )
    received = exchange(message, REP)
    return call(
        output_kernel,
        "output",
        (shape(1024, 256), shape(128, 256, dtype=F32), shape(1024, 128)),
        [SMEM, VMEM, VMEM],
    )(order, received, weight)


def solution(mesh):
    fine = Mesh(mesh.devices.reshape(4, 4, 4, 4, 2), REP + ROW)
    placed = (
        P(ROW, None),
        P(REP, ROW, None, None, None),
        P(REP, ROW, None),
        P(REP, ROW, None),
        P(),
        P(ROW, None),
    )
    return jax.shard_map(
        body,
        mesh=fine,
        in_specs=placed,
        out_specs=(P(ROW, None), P(), P(ROW, None)),
        check_vma=False,
    )
```

```python
import math

import jax
import jax.numpy as jnp
from jax import lax
from jax.experimental import pallas as pl
from jax.experimental.pallas import tpu as pltpu
from jax.sharding import Mesh
from jax.sharding import PartitionSpec as P

REP = ("zl", "x")
ROW = ("zh", "y", "c")
F32 = jnp.float32
BF16 = jnp.bfloat16
VMEM = pl.BlockSpec(memory_space=pltpu.VMEM)
SMEM = pl.BlockSpec(memory_space=pltpu.SMEM)
HBM = pl.BlockSpec(memory_space=pltpu.HBM)

NEAR = ((1, 2, 3, 0), (2, 3, 0, 1))


def farther(q, half):
    return 1 - (((q >> 1) + 1) >> 1 & 1) ^ half


def pair(q, zh, k):
    half, turn = k // 4, k % 2
    if k // 2 % 2 != farther(q, half):
        turn += 2
    a = NEAR[q // 8][(zh - half * 2 - q // 8) % 4] * 4 + (q + turn) % 4
    return a * 32 + q + half * 16, q * 32 + zh * 8 + k


def quarter_of(a, s):
    turn = (a - s) & 3
    far = farther(s & 15, s >> 4)
    return (far ^ turn >> 1) * 2 + (turn & 1)


PAIRS = [pair(q, zh, k) for q in range(16) for zh in range(4) for k in range(8)]


def shape(*dims, dtype=BF16):
    return jax.ShapeDtypeStruct(dims, dtype)


def fill(counts, cols, tiles, dense, loads=()):
    def clear(b, carry):
        dense[pl.ds(pl.multiple_of(b * 128, 128), 128), :] = jnp.zeros((128, 2048), BF16)
        return carry

    lax.fori_loop(0, 8, clear, 0)
    yield
    start = jnp.int32(0)
    for b in range(8):
        if loads:
            loads[b].wait()
        count = counts[b]

        def place(i, carry, b=b, start=start):
            slot = start + i
            col = pl.multiple_of(cols[slot] * 128, 128)
            dense[b * 128 : (b + 1) * 128, pl.ds(col, 128)] = tiles[slot]
            return carry

        lax.fori_loop(0, count, place, 0)
        start = start + count
    yield


def tile_copies(tiles_hbm, tiles, sems):
    return [
        pltpu.make_async_copy(
            tiles_hbm.at[pl.ds(i * 12, 12)], tiles.at[pl.ds(i * 12, 12)], sems.at[i]
        )
        for i in range(8)
    ]


def backward_kernel(
    counts, cols, tiles_hbm, grad_hbm, weight_hbm, terms,
    tiles, node_grad, weight, dense, grad_t, sems,
):
    copies = [
        pltpu.make_async_copy(weight_hbm, weight, sems.at[8]),
        pltpu.make_async_copy(grad_hbm, node_grad, sems.at[9]),
    ]
    loads = tile_copies(tiles_hbm, tiles, sems)
    for copy in copies + loads:
        copy.start()
    filling = fill(counts, cols, tiles, dense, loads)
    next(filling)
    copies[0].wait()
    copies[1].wait()
    grad_t[...] = lax.dot_general(
        weight[...], node_grad[...], (((1,), (1,)), ((), ())), preferred_element_type=F32
    ).astype(BF16)
    next(filling)
    for k in range(8):
        term = jnp.dot(
            grad_t[...], dense[:, k * 256 : (k + 1) * 256], preferred_element_type=F32
        )
        terms[k % 2, k // 2] = term.T.astype(BF16)


def pack_kernel(terms, quarter, message):
    for y in range(4):
        message[y, 0:256, :] = quarter[...]
        message[y, 256:512, :] = (terms[0, y].astype(F32) + terms[1, y].astype(F32)).astype(BF16)


def split_kernel(received, held, column_sum):
    total = received[0, 256:512, :].astype(F32)
    for y in range(1, 4):
        total = total + received[y, 256:512, :].astype(F32)
    column_sum[...] = total.astype(BF16)
    for c in range(2):
        held[c] = received[:, 0:256, :]


def dense_kernel(counts, cols, tiles, dense):
    for _ in fill(counts, cols, tiles, dense):
        pass


def forward_kernel(scaling, dense, held, node_grad, message, total):
    for k in range(8):
        term = jnp.dot(
            dense[:, k * 256 : (k + 1) * 256], held[k % 2, k // 2], preferred_element_type=F32
        )
        if k == 0:
            total[...] = term
        else:
            total[...] += term
    partial = total[...].astype(BF16)
    message[:, 0:64, :] = partial.reshape(16, 64, 128)
    term = lax.dot_general(
        partial, node_grad[...], (((0,), (0,)), ((), ())), preferred_element_type=F32
    )
    term = term * scaling
    message[:, 64:80, :] = jnp.concatenate(
        [term[:, 0:128].reshape(16, 8, 128), term[:, 128:256].reshape(16, 8, 128)], axis=1
    ).astype(BF16)


def reduce_kernel(shard, parts, piece, weight_part):
    total = parts[0, 0:64, :].astype(F32)
    for a in range(1, 16):
        total = total + parts[a, 0:64, :].astype(F32)
    piece[0:64, :] = total.astype(BF16)
    for part in range(4):
        total = parts[part, 80:96, :].astype(F32)
        for zl in range(1, 4):
            total = total + parts[zl * 4 + part, 80:96, :].astype(F32)
        row = pl.multiple_of(64 + quarter_of(part, shard[0]) * 16, 16)
        piece[pl.ds(row, 16), :] = total.astype(BF16)
    total = parts[0, 64:80, :].astype(F32)
    for a in range(1, 16):
        total = total + parts[a, 64:80, :].astype(F32)
    weight_part[...] = jnp.broadcast_to(total.astype(BF16)[None], (32, 16, 128))


def gather_kernel(piece, weight_parts, message):
    message[:, 0:128, :] = jnp.broadcast_to(piece[...][None], (16, 128, 128))
    total = weight_parts[0].astype(F32)
    for r in range(1, 32):
        total = total + weight_parts[r].astype(F32)
    message[:, 128:144, :] = jnp.broadcast_to(total.astype(BF16)[None], (16, 16, 128))


def output_kernel(received, weight, output, weight_grad, feature_grad):
    parts = received[:, 128:144, :].astype(F32)
    weight_grad[:, 0:128] = parts[:, 0:8, :].reshape(128, 128)
    weight_grad[:, 128:256] = parts[:, 8:16, :].reshape(128, 128)
    for zq in range(4):
        aggregate = received[zq * 4 : zq * 4 + 4, 0:64, :].reshape(256, 128)
        output[zq * 256 : (zq + 1) * 256, :] = jnp.dot(
            aggregate, weight[...], preferred_element_type=F32
        ).astype(BF16)
        feature_grad[zq * 256 : (zq + 1) * 256, :] = received[
            :, 64 + zq * 16 : 80 + zq * 16, :
        ].reshape(256, 128)


def call(kernel, name, outs, ins, scratch=(), flops=0, moved=1 << 20, limit=16):
    return pl.pallas_call(
        kernel,
        out_shape=outs,
        in_specs=ins,
        out_specs=jax.tree.map(lambda _: VMEM, outs),
        scratch_shapes=list(scratch),
        compiler_params=pltpu.CompilerParams(vmem_limit_bytes=limit << 20),
        cost_estimate=pl.CostEstimate(flops=flops, bytes_accessed=moved, transcendentals=0),
        name=name,
    )


def exchange(block, axes):
    return lax.all_to_all(block, axes, 0, 0)


def body(features, tile_values, tile_counts, tile_columns, weight, node_grad):
    rep_index = lax.axis_index(REP)
    row_index = lax.axis_index(ROW)
    scaling = 1.0 / math.sqrt(features.shape[0] * 32)
    counts, cols, tiles = tile_counts[0, 0], tile_columns[0, 0], tile_values[0, 0]
    shard = row_index.astype(jnp.int32).reshape(1)

    terms = call(
        backward_kernel,
        "backward",
        shape(2, 4, 256, 128),
        [SMEM, SMEM, HBM, HBM, HBM],
        [
            pltpu.VMEM((96, 128, 128), BF16),
            pltpu.VMEM((1024, 256), BF16),
            pltpu.VMEM((128, 256), BF16),
            pltpu.VMEM((1024, 2048), BF16),
            pltpu.VMEM((128, 1024), BF16),
            pltpu.SemaphoreType.DMA((10,)),
        ],
        flops=2 * 128 * 1024 * 2304,
        moved=8 << 20,
        limit=58,
    )(counts, cols, tiles, node_grad, weight)
    start = quarter_of(rep_index, row_index) * 256
    quarter = lax.dynamic_slice_in_dim(features, start, 256, axis=0)
    quarter = lax.ppermute(quarter, REP + ROW, PAIRS)
    terms = exchange(terms, "c")
    message = call(pack_kernel, "pack", shape(4, 512, 128), [VMEM] * 2)(terms, quarter)
    received = exchange(message, "y")

    held, column_sum = call(
        split_kernel, "split", (shape(2, 4, 256, 128), shape(256, 128)), [VMEM]
    )(received)
    column_sum = lax.ppermute(column_sum, REP + ROW, [(d, s) for s, d in PAIRS])
    dense = call(dense_kernel, "dense", shape(1024, 2048), [SMEM, SMEM, VMEM])(
        counts, cols, tiles
    )
    held, dense = lax.optimization_barrier((held, dense))
    held = exchange(held, "c")
    message = call(
        lambda *refs: forward_kernel(scaling, *refs),
        "forward",
        shape(16, 80, 128),
        [VMEM] * 3,
        [pltpu.VMEM((1024, 128), F32)],
        flops=2 * 128 * 1024 * 2304,
        moved=3 << 20,
    )(dense, held, node_grad)
    message = jnp.concatenate([message, column_sum.reshape(16, 16, 128)], axis=1)
    parts = exchange(message, REP)

    piece, weight_part = call(
        reduce_kernel, "reduce", (shape(128, 128), shape(32, 16, 128)), [SMEM, VMEM]
    )(shard, parts)
    weight_parts = exchange(weight_part, ROW)
    message = call(gather_kernel, "gather", shape(16, 144, 128), [VMEM] * 2)(piece, weight_parts)
    received = exchange(message, REP)
    return call(
        output_kernel,
        "output",
        (shape(1024, 256), shape(128, 256, dtype=F32), shape(1024, 128)),
        [VMEM, VMEM],
    )(received, weight)


def solution(mesh):
    fine = Mesh(mesh.devices.reshape(4, 4, 4, 4, 2), REP + ROW)
    placed = (
        P(ROW, None),
        P(REP, ROW, None, None, None),
        P(REP, ROW, None),
        P(REP, ROW, None),
        P(),
        P(ROW, None),
    )
    return jax.shard_map(
        body,
        mesh=fine,
        in_specs=placed,
        out_specs=(P(ROW, None), P(), P(ROW, None)),
        check_vma=False,
    )
```

```python
import math

import jax
import jax.numpy as jnp
from jax import lax
from jax.experimental import pallas as pl
from jax.experimental.pallas import tpu as pltpu
from jax.sharding import Mesh
from jax.sharding import PartitionSpec as P

REP = ("zl", "x")
ROW = ("zh", "y", "c")
F32 = jnp.float32
BF16 = jnp.bfloat16
VMEM = pl.BlockSpec(memory_space=pltpu.VMEM)
SMEM = pl.BlockSpec(memory_space=pltpu.SMEM)
HBM = pl.BlockSpec(memory_space=pltpu.HBM)

NEAR = ((1, 2, 3, 0), (2, 3, 0, 1))


def farther(q, half):
    return 1 - (((q >> 1) + 1) >> 1 & 1) ^ half


def pair(q, zh, k):
    half, turn = k // 4, k % 2
    if k // 2 % 2 != farther(q, half):
        turn += 2
    a = NEAR[q // 8][(zh - half * 2 - q // 8) % 4] * 4 + (q + turn) % 4
    return a * 32 + q + half * 16, q * 32 + zh * 8 + k


def quarter_of(a, s):
    turn = (a - s) & 3
    far = farther(s & 15, s >> 4)
    return (far ^ turn >> 1) * 2 + (turn & 1)


PAIRS = [pair(q, zh, k) for q in range(16) for zh in range(4) for k in range(8)]


def shape(*dims, dtype=BF16):
    return jax.ShapeDtypeStruct(dims, dtype)


def fill(counts, cols, tiles, dense, loads=()):
    def clear(b, carry):
        dense[pl.ds(pl.multiple_of(b * 128, 128), 128), :] = jnp.zeros((128, 2048), BF16)
        return carry

    lax.fori_loop(0, 8, clear, 0)
    yield
    start = jnp.int32(0)
    for b in range(8):
        if loads:
            loads[b].wait()
        count = counts[b]

        def place(i, carry, b=b, start=start):
            slot = start + i
            col = pl.multiple_of(cols[slot] * 128, 128)
            dense[b * 128 : (b + 1) * 128, pl.ds(col, 128)] = tiles[slot]
            return carry

        lax.fori_loop(0, count, place, 0)
        start = start + count
    yield


def tile_copies(tiles_hbm, tiles, sems):
    return [
        pltpu.make_async_copy(
            tiles_hbm.at[pl.ds(i * 12, 12)], tiles.at[pl.ds(i * 12, 12)], sems.at[i]
        )
        for i in range(8)
    ]


def backward_kernel(
    counts, cols, tiles_hbm, grad_hbm, weight_hbm, terms,
    tiles, node_grad, weight, dense, grad_t, sems,
):
    copies = [
        pltpu.make_async_copy(weight_hbm, weight, sems.at[8]),
        pltpu.make_async_copy(grad_hbm, node_grad, sems.at[9]),
    ]
    loads = tile_copies(tiles_hbm, tiles, sems)
    for copy in copies + loads:
        copy.start()
    filling = fill(counts, cols, tiles, dense, loads)
    next(filling)
    copies[0].wait()
    copies[1].wait()
    grad_t[...] = lax.dot_general(
        weight[...], node_grad[...], (((1,), (1,)), ((), ())), preferred_element_type=F32
    ).astype(BF16)
    next(filling)
    for k in range(8):
        term = jnp.dot(
            grad_t[...], dense[:, k * 256 : (k + 1) * 256], preferred_element_type=F32
        )
        terms[k % 2, k // 2] = term.T.astype(BF16)


def pack_kernel(terms, quarter, message):
    for y in range(4):
        message[y, 0:256, :] = quarter[...]
        message[y, 256:512, :] = (terms[0, y].astype(F32) + terms[1, y].astype(F32)).astype(BF16)


def split_kernel(received, held, column_sum):
    total = received[0, 256:512, :].astype(F32)
    for y in range(1, 4):
        total = total + received[y, 256:512, :].astype(F32)
    column_sum[...] = total.astype(BF16)
    for c in range(2):
        held[c] = received[:, 0:256, :]


def forward_kernel(scaling, counts, cols, tiles, held, node_grad, message, dense, total):
    for _ in fill(counts, cols, tiles, dense):
        pass
    for k in range(8):
        term = jnp.dot(
            dense[:, k * 256 : (k + 1) * 256], held[k % 2, k // 2], preferred_element_type=F32
        )
        if k == 0:
            total[...] = term
        else:
            total[...] += term
    partial = total[...].astype(BF16)
    message[:, 0:64, :] = partial.reshape(16, 64, 128)
    term = lax.dot_general(
        partial, node_grad[...], (((0,), (0,)), ((), ())), preferred_element_type=F32
    )
    term = term * scaling
    message[:, 64:80, :] = jnp.concatenate(
        [term[:, 0:128].reshape(16, 8, 128), term[:, 128:256].reshape(16, 8, 128)], axis=1
    ).astype(BF16)


def reduce_kernel(shard, parts, piece, weight_part):
    total = parts[0, 0:64, :].astype(F32)
    for a in range(1, 16):
        total = total + parts[a, 0:64, :].astype(F32)
    piece[0:64, :] = total.astype(BF16)
    for part in range(4):
        total = parts[part, 80:96, :].astype(F32)
        for zl in range(1, 4):
            total = total + parts[zl * 4 + part, 80:96, :].astype(F32)
        row = pl.multiple_of(64 + quarter_of(part, shard[0]) * 16, 16)
        piece[pl.ds(row, 16), :] = total.astype(BF16)
    total = parts[0, 64:80, :].astype(F32)
    for a in range(1, 16):
        total = total + parts[a, 64:80, :].astype(F32)
    weight_part[...] = jnp.broadcast_to(total.astype(BF16)[None], (32, 16, 128))


def gather_kernel(piece, weight_parts, message):
    message[:, 0:128, :] = jnp.broadcast_to(piece[...][None], (16, 128, 128))
    total = weight_parts[0].astype(F32)
    for r in range(1, 32):
        total = total + weight_parts[r].astype(F32)
    message[:, 128:144, :] = jnp.broadcast_to(total.astype(BF16)[None], (16, 16, 128))


def output_kernel(received, weight, output, weight_grad, feature_grad):
    parts = received[:, 128:144, :].astype(F32)
    weight_grad[:, 0:128] = parts[:, 0:8, :].reshape(128, 128)
    weight_grad[:, 128:256] = parts[:, 8:16, :].reshape(128, 128)
    for zq in range(4):
        aggregate = received[zq * 4 : zq * 4 + 4, 0:64, :].reshape(256, 128)
        output[zq * 256 : (zq + 1) * 256, :] = jnp.dot(
            aggregate, weight[...], preferred_element_type=F32
        ).astype(BF16)
        feature_grad[zq * 256 : (zq + 1) * 256, :] = received[
            :, 64 + zq * 16 : 80 + zq * 16, :
        ].reshape(256, 128)


def call(kernel, name, outs, ins, scratch=(), flops=0, moved=1 << 20, limit=16):
    return pl.pallas_call(
        kernel,
        out_shape=outs,
        in_specs=ins,
        out_specs=jax.tree.map(lambda _: VMEM, outs),
        scratch_shapes=list(scratch),
        compiler_params=pltpu.CompilerParams(vmem_limit_bytes=limit << 20),
        cost_estimate=pl.CostEstimate(flops=flops, bytes_accessed=moved, transcendentals=0),
        name=name,
    )


def exchange(block, axes):
    return lax.all_to_all(block, axes, 0, 0)


def body(features, tile_values, tile_counts, tile_columns, weight, node_grad):
    rep_index = lax.axis_index(REP)
    row_index = lax.axis_index(ROW)
    scaling = 1.0 / math.sqrt(features.shape[0] * 32)
    counts, cols, tiles = tile_counts[0, 0], tile_columns[0, 0], tile_values[0, 0]
    shard = row_index.astype(jnp.int32).reshape(1)

    terms = call(
        backward_kernel,
        "backward",
        shape(2, 4, 256, 128),
        [SMEM, SMEM, HBM, HBM, HBM],
        [
            pltpu.VMEM((96, 128, 128), BF16),
            pltpu.VMEM((1024, 256), BF16),
            pltpu.VMEM((128, 256), BF16),
            pltpu.VMEM((1024, 2048), BF16),
            pltpu.VMEM((128, 1024), BF16),
            pltpu.SemaphoreType.DMA((10,)),
        ],
        flops=2 * 128 * 1024 * 2304,
        moved=8 << 20,
        limit=58,
    )(counts, cols, tiles, node_grad, weight)
    start = quarter_of(rep_index, row_index) * 256
    quarter = lax.dynamic_slice_in_dim(features, start, 256, axis=0)
    quarter = lax.ppermute(quarter, REP + ROW, PAIRS)
    terms = exchange(terms, "c")
    message = call(pack_kernel, "pack", shape(4, 512, 128), [VMEM] * 2)(terms, quarter)
    received = exchange(message, "y")

    held, column_sum = call(
        split_kernel, "split", (shape(2, 4, 256, 128), shape(256, 128)), [VMEM]
    )(received)
    column_sum = lax.ppermute(column_sum, REP + ROW, [(d, s) for s, d in PAIRS])
    held = exchange(held, "c")
    message = call(
        lambda *refs: forward_kernel(scaling, *refs),
        "forward",
        shape(16, 80, 128),
        [SMEM, SMEM] + [VMEM] * 3,
        [pltpu.VMEM((1024, 2048), BF16), pltpu.VMEM((1024, 128), F32)],
        flops=2 * 128 * 1024 * 2304,
        moved=3 << 20,
    )(counts, cols, tile_values[0, 0], held, node_grad)
    message = jnp.concatenate([message, column_sum.reshape(16, 16, 128)], axis=1)
    parts = exchange(message, REP)

    piece, weight_part = call(
        reduce_kernel, "reduce", (shape(128, 128), shape(32, 16, 128)), [SMEM, VMEM]
    )(shard, parts)
    weight_parts = exchange(weight_part, ROW)
    message = call(gather_kernel, "gather", shape(16, 144, 128), [VMEM] * 2)(piece, weight_parts)
    received = exchange(message, REP)
    return call(
        output_kernel,
        "output",
        (shape(1024, 256), shape(128, 256, dtype=F32), shape(1024, 128)),
        [VMEM, VMEM],
    )(received, weight)


def solution(mesh):
    fine = Mesh(mesh.devices.reshape(4, 4, 4, 4, 2), REP + ROW)
    placed = (
        P(ROW, None),
        P(REP, ROW, None, None, None),
        P(REP, ROW, None),
        P(REP, ROW, None),
        P(),
        P(ROW, None),
    )
    return jax.shard_map(
        body,
        mesh=fine,
        in_specs=placed,
        out_specs=(P(ROW, None), P(), P(ROW, None)),
        check_vma=False,
    )
```
